512 devices in a mesh: site: 16 (over z, core), sector: 32 (over y, x).
Axes of the slice: x: 4, y: 8, z: 8, core: 2. Of those that a mesh axis runs over, the one named last changes fastest.
Arguments:
- left_env: bfloat16 [32, 128, 128], P('sector'), may hold values from -4 to 4
- mps_bra: bfloat16 [16, 512, 128, 128], P('site', 'sector'), may hold values from -0.5 to 0.5
- mps_ket: bfloat16 [16, 512, 128, 128], P('site', 'sector'), may hold values from -0.5 to 0.5
- joining_out: int32 [16, 512, 1], P('site', 'sector'), may hold values from 0 to 31; in each aligned block of 16 rows (0 to 15, 16 to 31, ..., all dimensions but the last counted through in order) at most 2 rows name the same one
- joining_mpo: int32 [16, 512], P('site', 'sector'), may hold values from 0 to 7
- owner: int32 [32], replicated, may hold values from 0 to 31, each once
- mpo_weight: float32 [16, 8], P('site'), may hold values from -1.5 to 1.5
Outputs:
- envs: bfloat16 [16, 32, 128, 128], P('site', 'sector')
The draws below stay inside these ranges and needn't reach their ends.
Inputs may be any that keep to these rules, and one draw needn't show every extreme that they name: `joining_out`: at each site, among the 16 triples of one input slot at most 2 name the same output slot.
All inputs are finite; a program needn't handle non-finite values.
Results may differ from the reference program's by a relative error of at most 0.04.
Values may be sent and summed in bfloat16 or wider, within the bound.
A program may use at most 64 MiB of HBM per device.

```python
import math
import jax
import jax.numpy as jnp
import numpy as np
from jax import lax

TILE = 128
TRIP = 16
CAP = 2
MPO_TERMS = 8
SECTORS = 32
SITES = 16


def set_ends(values, key, low, top_value):
    longest = values.shape.index(max(values.shape))
    spots = []
    for shift in (0, 1):
        where = [jax.random.randint(jax.random.fold_in(key, axis), (), 0, length) for axis, length in enumerate(values.shape)]
        where[longest] = (where[longest] + shift) % values.shape[longest]
        spots.append(tuple(where))
    return values.at[spots[0]].set(low).at[spots[1]].set(top_value)


def level_of(rng, extent, pieces, smallest, high):
    loudness, own = 1.0, jax.random.fold_in(rng, 6)
    for position, blocks in pieces:
        draws = jnp.exp(jax.random.uniform(jax.random.fold_in(own, position), (blocks,), jnp.float32, smallest / len(pieces), high / len(pieces)))
        loudness = loudness * jnp.repeat(draws, extent[position] // blocks).reshape([-1 if axis == position else 1 for axis in range(len(extent))])
    return loudness


def assign_block(rng, own, number, rows, number_of, top, bound, slope):
    order = jax.random.permutation(rng, number_of)
    crowded, ordinary = load_shares(number_of, rows * top, bound, slope, True), load_shares(number_of, rows * top, bound, slope, False)
    places = jnp.arange(number_of)

    def named(tallies, rotation):
        used = int((tallies > 0).sum())
        fixed = max(1, used // 4)
        passed = fixed + (places - fixed + rotation * (used - fixed)) % max(1, number_of - fixed)
        return jnp.zeros((number_of,), jnp.int32).at[order[jnp.where(places < fixed, places, passed)]].set(jnp.asarray(tallies, jnp.int32))

    tallies = jnp.where(number % 4 == 0, named(crowded, number // 4), named(ordinary, number - number // 4 - 1))
    mixed = jax.random.permutation(jax.random.fold_in(own, 3), number_of)
    giver, taker = mixed[0:number_of // 2 * 2:2], mixed[1:number_of // 2 * 2:2]
    slack = jnp.minimum(tallies[giver] - 1, bound - tallies[taker]) // 2
    slack = jnp.where((giver == order[0]) | (taker == order[0]) | (tallies[taker] == 0), 0, jnp.maximum(slack, 0))
    passed = jax.random.randint(jax.random.fold_in(own, 4), (number_of // 2,), 0, 1 << 20) % (slack + 1)
    tallies = tallies.at[giver].add(-passed).at[taker].add(passed)
    members = jnp.searchsorted(jnp.cumsum(tallies), jnp.arange(rows * top), side="right").astype(jnp.int32)
    table = members.reshape(top, rows).T
    table = table[jax.random.permutation(jax.random.fold_in(own, 1), rows)]
    rotation = jax.random.randint(jax.random.fold_in(own, 2), (rows, 1), 0, top)
    return jnp.take_along_axis(table, (jnp.arange(top)[None, :] + rotation) % top, axis=1)


def load_shares(amount, total, most, slope, full):
    portions = [(1 << 20) // math.isqrt(rank ** slope) + 1 for rank in range(1, amount + 1)]
    largest = most if full else min(most, max(-(-total // amount), total * portions[0] // sum(portions)))
    least = 1 if total - largest >= amount - 1 else 0
    holding, surplus = [largest] + [least] * (amount - 1), total - largest - least * (amount - 1)
    while surplus > 0:
        free = [i for i in range(1, amount) if holding[i] < largest] or [i for i in range(1, amount) if holding[i] < most]
        whole, budget = sum([portions[i] for i in free]), surplus
        for i in free:
            more = min(most - holding[i], max(1, budget * portions[i] // whole), surplus)
            holding[i] = holding[i] + more
            surplus = surplus - more
    return np.array(holding)


def centred(key, dims, deviation, bound, pieces=(), held_as=jnp.bfloat16):
    gain = level_of(key, dims, pieces, -0.22, 0.18) if pieces else 1.0
    values = jax.random.normal(key, dims, jnp.float32) * deviation * gain
    return jnp.minimum(jnp.maximum(values, -bound), bound).astype(held_as)


def setup_inputs(seed: int = 0) -> dict:
    key_list = jax.random.split(jax.random.key(seed), 8)
    left_env = centred(key_list[0], (SECTORS, TILE, TILE), 0.3, 4.0, ((0, 32),))
    mps_bra = centred(key_list[1], (SITES, SECTORS * TRIP, TILE, TILE), TILE ** -0.5, 0.5, ((0, 16), (1, 32)))
    mps_ket = centred(key_list[2], (SITES, SECTORS * TRIP, TILE, TILE), TILE ** -0.5, 0.5, ((0, 16), (1, 32)))
    joining_out_keys = jax.random.split(jax.random.fold_in(key_list[3], 1), SITES * (SECTORS * TRIP) // TRIP)
    joining_out_turns = jax.random.permutation(jax.random.fold_in(key_list[3], 3), SITES * (SECTORS * TRIP) // TRIP)
    joining_out = jax.vmap(lambda own, number: assign_block(jax.random.fold_in(key_list[3], 2), own, number, TRIP, SECTORS, 1, CAP, 2))(joining_out_keys, joining_out_turns).reshape((SITES, SECTORS * TRIP, 1))
    joining_mpo = set_ends(jax.random.randint(key_list[4], (SITES, SECTORS * TRIP), 0, MPO_TERMS), jax.random.fold_in(key_list[4], 1), 0, MPO_TERMS - 1).astype(jnp.int32)
    owner = jax.random.permutation(key_list[5], SECTORS).astype(jnp.int32)
    mpo_weight = centred(key_list[6], (SITES, MPO_TERMS), TRIP ** -0.5, 1.5, ((0, 16),), jnp.float32)
    return dict(left_env=left_env, mps_bra=mps_bra, mps_ket=mps_ket, joining_out=joining_out, joining_mpo=joining_mpo, owner=owner, mpo_weight=mpo_weight)


def reference(left_env, mps_bra, mps_ket, joining_out, joining_mpo, owner, mpo_weight):
    slot_ids = jnp.arange(SECTORS, dtype=jnp.int32)
    current = left_env
    stacked = [left_env]
    for site_step in range(SITES - 1):
        bra_tiles = mps_bra[site_step].reshape(SECTORS, TRIP, TILE, TILE).astype(jnp.float32)
        ket_tiles = mps_ket[site_step].reshape(SECTORS, TRIP, TILE, TILE).astype(jnp.float32)
        inner_part = jnp.einsum("dab,dkbc->dkac", current.astype(jnp.float32), ket_tiles)
        inner_part = lax.optimization_barrier(inner_part.astype(jnp.bfloat16)).astype(jnp.float32)
        product = jnp.einsum("dkai,dkac->dkic", bra_tiles, inner_part)
        target = owner[joining_out[site_step, :, 0]].reshape(SECTORS, TRIP)
        weights = mpo_weight[site_step][joining_mpo[site_step]].reshape(SECTORS, TRIP)
        routing = (target[:, :, None] == slot_ids[None, None, :]).astype(jnp.float32) * weights[:, :, None]
        partial_value = jnp.einsum("dke,dkic->deic", routing, product)
        partial_value = lax.optimization_barrier(partial_value.astype(jnp.bfloat16)).astype(jnp.float32)
        current = jnp.sum(partial_value, axis=0).astype(jnp.bfloat16)
        stacked.append(current)
    return jnp.stack(stacked)
```

```python
import functools

import jax
import jax.numpy as jnp
from jax import lax
from jax.experimental import pallas as pl
from jax.experimental.pallas import tpu as pltpu
from jax.sharding import PartitionSpec as P

MESH = pl.DeviceIdType.MESH
BF16 = jnp.bfloat16
F32 = jnp.float32

NX, NY, NZ = 4, 8, 8
SLOTS = NX * NY
STEPS = 15
TRIP = 16
ROWS = 16
TILE = 128


def hops(offset):
    dy, dx = offset
    return min(dy, NY - dy) + min(dx, NX - dx)


PLANE = sorted(
    [(dy, dx) for dy in range(NY) for dx in range(NX) if (dy, dx) != (0, 0)], key=hops, reverse=True
)
COLUMN = sorted(range(1, NZ), key=lambda d: min(d, NZ - d), reverse=True)
N_PLANE = len(PLANE)
N_COLUMN = len(COLUMN)


def chain(
    env_ref, bt_ref, ket_ref, first_ref, second_ref, weight_ref, out_ref,
    env, prod, part, got, leave, land,
    part_send, part_recv, env_send, env_recv, out_send, out_recv,
):
    site = lax.axis_index("site")
    sector = lax.axis_index("sector")
    z, core = site // 2, lax.rem(site, 2)
    y, x = sector // NX, lax.rem(sector, NX)

    def slot_at(offset):
        return lax.rem(y + offset[0], NY) * NX + lax.rem(x + offset[1], NX)

    def site_at(d):
        return lax.rem(z + d, NZ) * 2 + 1

    barrier = pltpu.get_barrier_semaphore()
    pl.semaphore_signal(barrier, inc=1, device_id=(z * 2 + 1 - core, sector), device_id_type=MESH)

    @pl.when(core == 0)
    def _():
        pl.semaphore_wait(barrier, 1)

        @pl.when(z == 0)
        def _():
            out_ref[...] = env_ref[...]

        @pl.when(z > 0)
        def _():
            pltpu.make_async_remote_copy(
                src_ref=leave, dst_ref=land, send_sem=out_send, recv_sem=out_recv,
                device_id=(site + 1, sector), device_id_type=MESH,
            ).wait_recv()
            out_ref[...] = land[...]

    @pl.when(core == 1)
    def _():
        for offset in PLANE:
            pl.semaphore_signal(barrier, inc=1, device_id=(site, slot_at(offset)), device_id_type=MESH)
        for d in COLUMN:
            pl.semaphore_signal(barrier, inc=1, device_id=(site_at(d), sector), device_id_type=MESH)
        pl.semaphore_wait(barrier, 1 + N_PLANE + N_COLUMN)

        env[0] = env_ref[...]
        prod[TRIP] = jnp.zeros((ROWS, TILE), F32)
        rows = pl.ds(pl.multiple_of(z * ROWS, ROWS), ROWS)

        def send_part(p, i):
            return pltpu.make_async_remote_copy(
                src_ref=part.at[p, i], dst_ref=got.at[p, i],
                send_sem=part_send.at[p], recv_sem=part_recv.at[p],
                device_id=(site, slot_at(PLANE[i])), device_id_type=MESH,
            )

        def all_parts(p):
            return pltpu.make_async_remote_copy(
                src_ref=part.at[p, pl.ds(0, N_PLANE)], dst_ref=got.at[p, pl.ds(0, N_PLANE)],
                send_sem=part_send.at[p], recv_sem=part_recv.at[p],
                device_id=(site, slot_at(PLANE[0])), device_id_type=MESH,
            )

        def send_rows(q, d):
            return pltpu.make_async_remote_copy(
                src_ref=env.at[q, rows], dst_ref=env.at[q, rows],
                send_sem=env_send.at[q], recv_sem=env_recv.at[q],
                device_id=(site_at(d), sector), device_id_type=MESH,
            )

        def all_rows(q):
            span = pl.ds(0, N_COLUMN * ROWS)
            return pltpu.make_async_remote_copy(
                src_ref=env.at[q, span], dst_ref=env.at[q, span],
                send_sem=env_send.at[q], recv_sem=env_recv.at[q],
                device_id=(site_at(COLUMN[0]), sector), device_id_type=MESH,
            )

        def to_core_0():
            return pltpu.make_async_remote_copy(
                src_ref=leave, dst_ref=land, send_sem=out_send, recv_sem=out_recv,
                device_id=(z * 2, sector), device_id_type=MESH,
            )

        def step(j, carry):
            p = lax.rem(j, 2)

            @pl.when(j > 0)
            def _():
                all_rows(p).wait_recv()

            left = jnp.dot(bt_ref[j], env[p], preferred_element_type=F32)
            for k in range(TRIP):
                scaled = (left[k * ROWS:(k + 1) * ROWS] * weight_ref[j * TRIP + k]).astype(BF16)
                prod[k] = jnp.dot(scaled, ket_ref[j, k], preferred_element_type=F32)

            def summed(slot):
                at = j * SLOTS + slot
                return (prod[first_ref[at]] + prod[second_ref[at]]).astype(BF16)

            for i in range(N_PLANE):
                part[p, i] = summed(slot_at(PLANE[i]))
                send_part(p, i).start()
            got[p, N_PLANE] = summed(sector)

            @pl.when(j > 0)
            def _():
                all_parts(1 - p).wait_send()
                all_rows(p).wait_send()

            @pl.when((j > 0) & (j == z * 2))
            def _():
                leave[...] = env[p]
                to_core_0().start()

            @pl.when(j == site)
            def _():
                out_ref[...] = env[p]

            all_parts(p).wait_recv()
            total = got[p, 0].astype(F32)
            for i in range(1, SLOTS):
                total += got[p, i].astype(F32)
            env[1 - p, rows] = total.astype(BF16)
            for d in COLUMN:
                send_rows(1 - p, d).start()
            return carry

        lax.fori_loop(0, STEPS, step, 0)
        last = STEPS % 2
        all_rows(last).wait_recv()

        @pl.when(site == STEPS)
        def _():
            out_ref[...] = env[last]

        all_rows(last).wait_send()
        all_parts(1 - last).wait_send()

        @pl.when(z > 0)
        def _():
            to_core_0().wait_send()


def run_chain(env, bt, ket, first, second, weight):
    vmem = pl.BlockSpec(memory_space=pltpu.VMEM)
    smem = pl.BlockSpec(memory_space=pltpu.SMEM)
    dma = pltpu.SemaphoreType.DMA
    return pl.pallas_call(
        chain,
        out_shape=jax.ShapeDtypeStruct((TILE, TILE), BF16),
        in_specs=[vmem, vmem, vmem, smem, smem, smem],
        out_specs=vmem,
        scratch_shapes=[
            pltpu.VMEM((2, TILE, TILE), BF16),
            pltpu.VMEM((TRIP + 1, ROWS, TILE), F32),
            pltpu.VMEM((2, N_PLANE, ROWS, TILE), BF16),
            pltpu.VMEM((2, SLOTS, ROWS, TILE), BF16),
            pltpu.VMEM((TILE, TILE), BF16),
            pltpu.VMEM((TILE, TILE), BF16),
            dma((2,)), dma((2,)), dma((2,)), dma((2,)), dma, dma,
        ],
        compiler_params=pltpu.CompilerParams(
            collective_id=0, has_side_effects=True, vmem_limit_bytes=40 << 20
        ),
        name="chain",
    )(env, bt, ket, first, second, weight)


def lookups(joining_out, joining_mpo, owner, mpo_weight):
    slots = jnp.arange(SLOTS, dtype=jnp.int32)
    outputs = joining_out[0, :, 0]
    target = jnp.sum(jnp.where(outputs[:, None] == slots[None, :], owner[None, :], 0), axis=1)
    terms = jnp.arange(mpo_weight.shape[1], dtype=jnp.int32)
    weights = jnp.sum(
        jnp.where(joining_mpo[0][:, None] == terms[None, :], mpo_weight[0][None, :], 0.0), axis=1
    )
    place = jnp.arange(TRIP, dtype=jnp.int32)[:, None]
    hit = target[:, None] == slots[None, :]
    first = jnp.min(jnp.where(hit, place, TRIP), axis=0)
    second = jnp.min(jnp.where(hit & (place != first[None, :]), place, TRIP), axis=0)
    return first, second, weights


def local(left_env, mps_bra, mps_ket, joining_out, joining_mpo, owner, mpo_weight):
    first, second, weights = lookups(joining_out, joining_mpo, owner, mpo_weight)
    tables = lax.all_gather(jnp.concatenate([first, second]), "site")
    first, second = tables[:, :SLOTS].reshape(-1), tables[:, SLOTS:].reshape(-1)
    weights = lax.all_gather(weights, "site").reshape(-1)
    ket = lax.all_gather(mps_ket[0], "site")
    bt = mps_bra[0].transpose(0, 2, 1).reshape(TRIP, NZ, ROWS, TILE).transpose(1, 0, 2, 3)
    bt = jnp.repeat(bt.reshape(NZ, TRIP * ROWS, TILE), 2, axis=0)
    bt = lax.all_to_all(bt, "site", split_axis=0, concat_axis=0, tiled=True)
    return run_chain(left_env[0], bt, ket, first, second, weights)[None, None]


def solution(mesh):
    return jax.shard_map(
        local,
        mesh=mesh,
        in_specs=(
            P("sector", None, None),
            P("site", "sector", None, None),
            P("site", "sector", None, None),
            P("site", "sector", None),
            P("site", "sector"),
            P(),
            P("site", None),
        ),
        out_specs=P("site", "sector", None, None),
        check_vma=False,
    )
```

```python
import functools

import jax
import jax.numpy as jnp
from jax import lax
from jax.experimental import pallas as pl
from jax.experimental.pallas import tpu as pltpu
from jax.sharding import PartitionSpec as P

MESH = pl.DeviceIdType.MESH
BF16 = jnp.bfloat16
F32 = jnp.float32

NX, NY, NZ = 4, 8, 8
SLOTS = NX * NY
STEPS = 15
TRIP = 16
ROWS = 16
TILE = 128
PIECES = 4
PIECE = TRIP // PIECES


def hops(offset):
    dy, dx = offset
    return min(dy, NY - dy) + min(dx, NX - dx)


PLANE = sorted(
    [(dy, dx) for dy in range(NY) for dx in range(NX) if (dy, dx) != (0, 0)], key=hops, reverse=True
)
COLUMN = sorted(range(1, NZ), key=lambda d: min(d, NZ - d), reverse=True)
N_PLANE = len(PLANE)
N_COLUMN = len(COLUMN)


def chain(
    env_ref, bra_ref, ket_ref, table_ref, weight_ref, out_ref,
    env, prod, part, got, leave, land, bt_out, bt, first_out, first_in, kets, tables, lookup,
    part_send, part_recv, env_send, env_recv, out_send, out_recv, bt_send, bt_recv,
    first_send, first_recv, table_send, table_recv, local_sem,
    up_send, down_send, over_send, ket_recv,
):
    site = lax.axis_index("site")
    sector = lax.axis_index("sector")
    z, core = site // 2, lax.rem(site, 2)
    y, x = sector // NX, lax.rem(sector, NX)
    rows = pl.ds(pl.multiple_of(z * ROWS, ROWS), ROWS)

    def slot_at(offset):
        return lax.rem(y + offset[0], NY) * NX + lax.rem(x + offset[1], NX)

    def plane_at(d):
        return lax.rem(z + d, NZ)

    def remote(src, dst, send_sem, recv_sem, to_site, to_sector=sector):
        return pltpu.make_async_remote_copy(
            src_ref=src, dst_ref=dst, send_sem=send_sem, recv_sem=recv_sem,
            device_id=(to_site, to_sector), device_id_type=MESH,
        )

    barrier = pltpu.get_barrier_semaphore()

    def greet(to_site, to_sector=sector):
        pl.semaphore_signal(barrier, inc=1, device_id=(to_site, to_sector), device_id_type=MESH)

    def send_table(d):
        return remote(tables.at[site], tables.at[site], table_send, table_recv, plane_at(d) * 2 + 1)

    def send_bt(d):
        return remote(
            bt_out.at[plane_at(d)], bt.at[site], bt_send, bt_recv.at[site], plane_at(d) * 2 + 1
        )

    def send_first(d):
        return remote(
            first_out.at[plane_at(d)], first_in, first_send, first_recv, plane_at(d) * 2 + 1
        )

    def to_core_0():
        return remote(leave, land, out_send, out_recv, z * 2)

    def ket_piece(f, q, send_sem, to_site):
        held = kets.at[f, pl.ds(q * PIECE, PIECE)]
        return remote(held, held, send_sem, ket_recv.at[f, q], to_site)

    def whole_ket(f, send_sem):
        return remote(kets.at[f], kets.at[f], send_sem, ket_recv.at[f, 0], site + 1 - 2 * core)

    greet(z * 2 + 1 - core)
    for d in COLUMN:
        greet(plane_at(d) * 2 + 1)

    @pl.when(core == 0)
    def _():
        greet(plane_at(1) * 2)
        greet(plane_at(NZ - 1) * 2)

    @pl.when(core == 1)
    def _():
        for d in COLUMN:
            greet(plane_at(d) * 2)
        for offset in PLANE:
            greet(site, slot_at(offset))

    own_ket = pltpu.make_async_copy(ket_ref, kets.at[site], local_sem)
    own_ket.start()
    tables[site] = table_ref[...]
    for k in range(TRIP):
        turned = jnp.transpose(bra_ref[k].astype(F32)) * weight_ref[k]
        bt_out[:, k * ROWS:(k + 1) * ROWS, :] = turned.astype(BF16).reshape(NZ, ROWS, TILE)

    @pl.when(core == 0)
    def _():
        @pl.when(z == 0)
        def _():
            out_ref[...] = env_ref[...]
            for k in range(TRIP):
                span = pl.ds(k * ROWS, ROWS)
                left = jnp.dot(
                    bt_out[:, span, :].reshape(TILE, TILE), env_ref[...], preferred_element_type=F32
                )
                whole = jnp.dot(left.astype(BF16), ket_ref[k], preferred_element_type=F32)
                first_out[:, span, :] = whole.astype(BF16).reshape(NZ, ROWS, TILE)

        pl.semaphore_wait(barrier, N_COLUMN + 3)
        own_ket.wait()
        for d in COLUMN + [0]:
            send_table(d).start()

        @pl.when(z == 0)
        def _():
            for d in COLUMN + [0]:
                send_first(d).start()

        def ways(f):
            away = lax.rem(z - f // 2 + NZ, NZ)
            up = away < NZ // 2
            down = (away == 0) | (away > NZ // 2 + 1)
            over = (away > 0) | (f == site)
            return up, down, over

        def serve(f, carry):
            up, down, over = ways(f)

            @pl.when(f == site)
            def _():
                for d in COLUMN + [0]:
                    send_bt(d).start()

            for q in range(PIECES):
                @pl.when(f != site)
                def _():
                    ket_piece(f, q, up_send, z * 2 + 1).wait_recv()

                @pl.when(up)
                def _():
                    ket_piece(f, q, up_send, plane_at(1) * 2).start()

                @pl.when(down)
                def _():
                    ket_piece(f, q, down_send, plane_at(NZ - 1) * 2).start()

                @pl.when(over)
                def _():
                    held = kets.at[f, pl.ds(q * PIECE, PIECE)]
                    remote(held, held, over_send, ket_recv.at[f, 0], z * 2 + 1).start()
            return carry

        lax.fori_loop(1, STEPS, serve, 0)

        @pl.when(z > 0)
        def _():
            to_core_0().wait_recv()
            out_ref[...] = land[...]

        def settle(f, carry):
            up, down, over = ways(f)
            for way, sem in ((up, up_send), (down, down_send), (over, over_send)):
                @pl.when(way)
                def _():
                    whole_ket(f, sem).wait_send()
            return carry

        lax.fori_loop(1, STEPS, settle, 0)
        for d in COLUMN + [0]:
            send_table(d).wait_send()

        @pl.when(z == 0)
        def _():
            for d in COLUMN + [0]:
                send_first(d).wait_send()

        @pl.when(z > 0)
        def _():
            for d in COLUMN + [0]:
                send_bt(d).wait_send()

    @pl.when(core == 1)
    def _():
        prod[TRIP] = jnp.zeros((ROWS, TILE), F32)
        bt[site] = bt_out[z]
        pl.semaphore_wait(barrier, 1 + N_PLANE + 2 * N_COLUMN)
        own_ket.wait()
        for d in COLUMN:
            send_table(d).start()

        @pl.when(site < STEPS)
        def _():
            for q in range(PIECES):
                ket_piece(site, q, over_send, z * 2).start()

        def start_bt():
            for d in COLUMN:
                send_bt(d).start()

        @pl.when(site == 1)
        def _():
            start_bt()

        def send_part(p, i):
            return remote(
                part.at[p, i], got.at[p, i], part_send.at[p], part_recv.at[p], site, slot_at(PLANE[i])
            )

        def all_parts(p):
            span = pl.ds(0, N_PLANE)
            return remote(
                part.at[p, span], got.at[p, span], part_send.at[p], part_recv.at[p],
                site, slot_at(PLANE[0]),
            )

        def send_rows(q, d):
            held = env.at[q, rows]
            return remote(held, held, env_send.at[q], env_recv.at[q], plane_at(d) * 2 + 1)

        def all_rows(q):
            held = env.at[q, pl.ds(0, N_COLUMN * ROWS)]
            return remote(held, held, env_send.at[q], env_recv.at[q], plane_at(COLUMN[0]) * 2 + 1)

        def scatter(j, p):
            def summed(slot):
                return (prod[lookup[j, 0, slot]] + prod[lookup[j, 1, slot]]).astype(BF16)

            for i in range(N_PLANE):
                part[p, i] = summed(slot_at(PLANE[i]))
                send_part(p, i).start()
            got[p, N_PLANE] = summed(sector)

        def gather(p):
            all_parts(p).wait_recv()
            total = got[p, 0].astype(F32)
            for i in range(1, SLOTS):
                total += got[p, i].astype(F32)
            env[1 - p, rows] = total.astype(BF16)
            for d in COLUMN:
                send_rows(1 - p, d).start()

        arrived = tables.at[pl.ds(0, 2 * NZ - 1)]
        remote(arrived, arrived, table_send, table_recv, z * 2).wait_recv()
        fetch = pltpu.make_async_copy(tables, lookup, local_sem)
        fetch.start()
        remote(first_in, first_in, first_send, first_recv, z * 2).wait_recv()
        for k in range(TRIP):
            prod[k] = first_in[k * ROWS:(k + 1) * ROWS].astype(F32)
        fetch.wait()
        scatter(0, 0)

        @pl.when(site == 3)
        def _():
            start_bt()

        gather(0)

        def step(j, carry):
            p = lax.rem(j, 2)

            @pl.when(j != site)
            def _():
                remote(bt.at[j], bt.at[j], bt_send, bt_recv.at[j], z * 2).wait_recv()
                whole_ket(j, over_send).wait_recv()

            all_rows(p).wait_recv()
            left = jnp.dot(bt[j], env[p], preferred_element_type=F32).astype(BF16)
            for k in range(TRIP):
                prod[k] = jnp.dot(
                    left[k * ROWS:(k + 1) * ROWS], kets[j, k], preferred_element_type=F32
                )
            scatter(j, p)
            all_parts(1 - p).wait_send()
            all_rows(p).wait_send()

            @pl.when(j == z * 2)
            def _():
                leave[...] = env[p]
                to_core_0().start()

            @pl.when(j == site)
            def _():
                out_ref[...] = env[p]

            @pl.when((j == site - 3) & (site < STEPS))
            def _():
                start_bt()

            gather(p)
            return carry

        lax.fori_loop(1, STEPS, step, 0)
        last = STEPS % 2
        all_rows(last).wait_recv()

        @pl.when(site == STEPS)
        def _():
            out_ref[...] = env[last]

        all_rows(last).wait_send()
        all_parts(1 - last).wait_send()

        @pl.when(z > 0)
        def _():
            to_core_0().wait_send()

        @pl.when(site < STEPS)
        def _():
            whole_ket(site, over_send).wait_send()
            for d in COLUMN:
                send_bt(d).wait_send()

        for d in COLUMN:
            send_table(d).wait_send()


def run_chain(env, bra, ket, table, weight):
    vmem = pl.BlockSpec(memory_space=pltpu.VMEM)
    smem = pl.BlockSpec(memory_space=pltpu.SMEM)
    dma = pltpu.SemaphoreType.DMA
    return pl.pallas_call(
        chain,
        out_shape=jax.ShapeDtypeStruct((TILE, TILE), BF16),
        in_specs=[vmem, vmem, vmem, vmem, smem],
        out_specs=vmem,
        scratch_shapes=[
            pltpu.VMEM((2, TILE, TILE), BF16),
            pltpu.VMEM((TRIP + 1, ROWS, TILE), F32),
            pltpu.VMEM((2, N_PLANE, ROWS, TILE), BF16),
            pltpu.VMEM((2, SLOTS, ROWS, TILE), BF16),
            pltpu.VMEM((TILE, TILE), BF16),
            pltpu.VMEM((TILE, TILE), BF16),
            pltpu.VMEM((NZ, TRIP * ROWS, TILE), BF16),
            pltpu.VMEM((2 * NZ, TRIP * ROWS, TILE), BF16),
            pltpu.VMEM((NZ, TRIP * ROWS, TILE), BF16),
            pltpu.VMEM((TRIP * ROWS, TILE), BF16),
            pltpu.VMEM((2 * NZ, TRIP, TILE, TILE), BF16),
            pltpu.VMEM((2 * NZ, 8, TILE), jnp.int32),
            pltpu.SMEM((2 * NZ, 8, TILE), jnp.int32),
            dma((2,)), dma((2,)), dma((2,)), dma((2,)), dma, dma, dma, dma((2 * NZ,)),
            dma, dma, dma, dma, dma,
            dma, dma, dma, dma((2 * NZ, PIECES)),
        ],
        compiler_params=pltpu.CompilerParams(
            collective_id=0, has_side_effects=True, vmem_limit_bytes=40 << 20
        ),
        name="chain",
    )(env, bra, ket, table, weight)


def lookups(joining_out, joining_mpo, owner, mpo_weight):
    slots = jnp.arange(SLOTS, dtype=jnp.int32)
    outputs = joining_out[0, :, 0]
    target = jnp.sum(jnp.where(outputs[:, None] == slots[None, :], owner[None, :], 0), axis=1)
    terms = jnp.arange(mpo_weight.shape[1], dtype=jnp.int32)
    weights = jnp.sum(
        jnp.where(joining_mpo[0][:, None] == terms[None, :], mpo_weight[0][None, :], 0.0), axis=1
    )
    place = jnp.arange(TRIP, dtype=jnp.int32)[:, None]
    hit = target[:, None] == slots[None, :]
    first = jnp.min(jnp.where(hit, place, TRIP), axis=0)
    second = jnp.min(jnp.where(hit & (place != first[None, :]), place, TRIP), axis=0)
    return first, second, weights


def local(left_env, mps_bra, mps_ket, joining_out, joining_mpo, owner, mpo_weight):
    first, second, weights = lookups(joining_out, joining_mpo, owner, mpo_weight)
    table = jnp.pad(jnp.stack([first, second]), ((0, 6), (0, TILE - SLOTS)))
    return run_chain(left_env[0], mps_bra[0], mps_ket[0], table, weights)[None, None]


def solution(mesh):
    return jax.shard_map(
        local,
        mesh=mesh,
        in_specs=(
            P("sector", None, None),
            P("site", "sector", None, None),
            P("site", "sector", None, None),
            P("site", "sector", None),
            P("site", "sector"),
            P(),
            P("site", None),
        ),
        out_specs=P("site", "sector", None, None),
        check_vma=False,
    )
```

```python
import functools

import jax
import jax.numpy as jnp
from jax import lax
from jax.experimental import pallas as pl
from jax.experimental.pallas import tpu as pltpu
from jax.sharding import PartitionSpec as P

MESH = pl.DeviceIdType.MESH
BF16 = jnp.bfloat16
F32 = jnp.float32

NX, NY, NZ = 4, 8, 8
SLOTS = NX * NY
STEPS = 15
TRIP = 16
ROWS = 16
TILE = 128
PIECES = 16
PIECE = TRIP // PIECES


def hops(offset):
    dy, dx = offset
    return min(dy, NY - dy) + min(dx, NX - dx)


PLANE = sorted(
    [(dy, dx) for dy in range(NY) for dx in range(NX) if (dy, dx) != (0, 0)], key=hops, reverse=True
)
COLUMN = sorted(range(1, NZ), key=lambda d: min(d, NZ - d), reverse=True)
N_PLANE = len(PLANE)
N_COLUMN = len(COLUMN)


def chain(
    env_ref, bra_ref, ket_ref, outputs_ref, terms_ref, owner_ref, weight_ref, out_ref,
    bra, env, prod, part, got, leave, land, bt_out, bt, first_out, first_in, kets, tables, lookup,
    part_send, part_recv, env_send, env_recv, out_send, out_recv, bt_send, bt_recv,
    first_send, first_recv, table_send, table_recv, table_sem, local_sem,
    up_send, down_send, over_send, ket_recv,
):
    site = lax.axis_index("site")
    sector = lax.axis_index("sector")
    z, core = site // 2, lax.rem(site, 2)
    y, x = sector // NX, lax.rem(sector, NX)
    rows = pl.ds(pl.multiple_of(z * ROWS, ROWS), ROWS)

    def slot_at(offset):
        return lax.rem(y + offset[0], NY) * NX + lax.rem(x + offset[1], NX)

    def plane_at(d):
        return lax.rem(z + d, NZ)

    def remote(src, dst, send_sem, recv_sem, to_site, to_sector=sector):
        return pltpu.make_async_remote_copy(
            src_ref=src, dst_ref=dst, send_sem=send_sem, recv_sem=recv_sem,
            device_id=(to_site, to_sector), device_id_type=MESH,
        )

    barrier = pltpu.get_barrier_semaphore()

    def greet(to_site, to_sector=sector):
        pl.semaphore_signal(barrier, inc=1, device_id=(to_site, to_sector), device_id_type=MESH)

    def send_table(d):
        return remote(tables.at[site], tables.at[site], table_send, table_recv.at[site], plane_at(d) * 2 + 1)

    def send_bt(d):
        return remote(
            bt_out.at[plane_at(d)], bt.at[site], bt_send, bt_recv.at[site], plane_at(d) * 2 + 1
        )

    def send_first(d):
        return remote(
            first_out.at[plane_at(d)], first_in, first_send, first_recv, plane_at(d) * 2 + 1
        )

    def to_core_0():
        return remote(leave, land, out_send, out_recv, z * 2)

    def ket_piece(f, q, send_sem, to_site):
        held = kets.at[f, pl.ds(q * PIECE, PIECE)]
        return remote(held, held, send_sem, ket_recv.at[f, q], to_site)

    def whole_ket(f, send_sem, tiles=TRIP):
        held = kets.at[f, pl.ds(0, tiles)]
        return remote(held, held, send_sem, ket_recv.at[f, 0], site + 1 - 2 * core)

    own_ket = pltpu.make_async_copy(ket_ref, kets.at[site], local_sem.at[0])
    own_bra = pltpu.make_async_copy(bra_ref, bra, local_sem.at[1])
    own_ket.start()
    own_bra.start()
    @pl.when(core == 0)
    def _():
        greet(plane_at(1) * 2)
        greet(plane_at(NZ - 1) * 2)

        @pl.when(z > 0)
        def _():
            greet(site + 1)

        @pl.when((z == 1) | (z == NZ - 1))
        def _():
            greet(1)

    @pl.when(core == 1)
    def _():
        for offset in PLANE:
            greet(site, slot_at(offset))
        for d in COLUMN:
            greet(plane_at(d) * 2 + 1)
            greet(plane_at(d) * 2)
        greet(site - 1)

    lane = lax.broadcasted_iota(jnp.int32, (8, TILE), 1)
    first = jnp.full((8, TILE), TRIP, jnp.int32)
    second = first
    for k in reversed(range(TRIP)):
        hit = lane == owner_ref[outputs_ref[k]]
        second = jnp.where(hit, first, second)
        first = jnp.where(hit, k, first)
    upper = lax.broadcasted_iota(jnp.int32, (8, TILE), 0) == 0
    tables[site] = jnp.where(upper, first, second)

    own_bra.wait()
    for k in range(TRIP):
        turned = jnp.transpose(bra[k].astype(F32)) * weight_ref[terms_ref[k]]
        bt_out[:, k * ROWS:(k + 1) * ROWS, :] = turned.astype(BF16).reshape(NZ, ROWS, TILE)
    own_ket.wait()

    @pl.when(core == 0)
    def _():
        pl.semaphore_wait(barrier, N_COLUMN + 3)

        @pl.when(z == 0)
        def _():
            def chunk(i, carry):
                d = NZ // 2 + (1 - 2 * lax.rem(i, 2)) * ((i + 1) // 2)
                to = plane_at(d)
                left = jnp.dot(bt_out[to], env_ref[...], preferred_element_type=F32).astype(BF16)
                for k in range(TRIP):
                    span = pl.ds(k * ROWS, ROWS)
                    value = jnp.dot(
                        left[k * ROWS:(k + 1) * ROWS], kets[0, k], preferred_element_type=F32
                    )
                    first_out[to, span] = value.astype(BF16)
                send_table(d).start()
                send_first(d).start()
                return carry

            lax.fori_loop(0, NZ, chunk, 0)
            out_ref[...] = env_ref[...]

        @pl.when(z > 0)
        def _():
            for d in COLUMN + [0]:
                send_table(d).start()

        @pl.when(z > 0)
        def _():
            for q in range(PIECES):
                ket_piece(site, q, up_send, plane_at(1) * 2).start()
                ket_piece(site, q, down_send, plane_at(NZ - 1) * 2).start()
                held = kets.at[site, pl.ds(q * PIECE, PIECE)]
                remote(held, held, over_send, ket_recv.at[site, 0], z * 2 + 1).start()

        def serve(f, carry):
            away = lax.rem(z - f // 2 + NZ, NZ)

            @pl.when(f == site)
            def _():
                for d in COLUMN + [0]:
                    send_bt(d).start()

            @pl.when((f != site) & ((f != 1) | (z != 0)))
            def _():
                for q in range(PIECES):
                    ket_piece(f, q, up_send, z * 2 + 1).wait_recv()
                    if 2 * q < PIECES:
                        up, down = away < NZ // 2, (away == 0) | (away > NZ // 2 + 1)
                    else:
                        up, down = away < NZ // 2 - 1, (away == 0) | (away > NZ // 2)
                    held = kets.at[f, pl.ds(q * PIECE, PIECE)]

                    @pl.when(up)
                    def _():
                        ket_piece(f, q, up_send, plane_at(1) * 2).start()

                    @pl.when(down)
                    def _():
                        ket_piece(f, q, down_send, plane_at(NZ - 1) * 2).start()

                    @pl.when(away > 0)
                    def _():
                        remote(held, held, over_send, ket_recv.at[f, 0], z * 2 + 1).start()

            return carry

        lax.fori_loop(1, STEPS, serve, 0)

        @pl.when(z > 0)
        def _():
            to_core_0().wait_recv()
            out_ref[...] = land[...]

        def settle(f, carry):
            away = lax.rem(z - f // 2 + NZ, NZ)
            live = (f != 1) | (z != 0)

            @pl.when(live & (away < NZ // 2 - 1))
            def _():
                whole_ket(f, up_send).wait_send()

            @pl.when(live & (away == NZ // 2 - 1))
            def _():
                whole_ket(f, up_send, TRIP // 2).wait_send()

            @pl.when(live & ((away == 0) | (away > NZ // 2 + 1)))
            def _():
                whole_ket(f, down_send).wait_send()

            @pl.when(live & (away == NZ // 2 + 1))
            def _():
                whole_ket(f, down_send, TRIP // 2).wait_send()

            @pl.when((away > 0) | (f == site))
            def _():
                whole_ket(f, over_send).wait_send()

            return carry

        lax.fori_loop(1, STEPS, settle, 0)
        for d in COLUMN + [0]:
            send_table(d).wait_send()

        @pl.when(z == 0)
        def _():
            for d in COLUMN + [0]:
                send_first(d).wait_send()

        @pl.when(z > 0)
        def _():
            for d in COLUMN + [0]:
                send_bt(d).wait_send()

    @pl.when(core == 1)
    def _():
        prod[TRIP] = jnp.zeros((ROWS, TILE), F32)
        bt[site] = bt_out[z]
        pl.semaphore_wait(barrier, N_PLANE + N_COLUMN + jnp.where(z == 0, 2, 1))
        @pl.when(site < STEPS)
        def _():
            for d in COLUMN:
                send_table(d).start()

        @pl.when((site > 1) & (site < STEPS))
        def _():
            for q in range(PIECES):
                ket_piece(site, q, over_send, z * 2).start()

        def start_bt():
            for d in COLUMN:
                send_bt(d).start()

        @pl.when(site == 1)
        def _():
            for q in range(PIECES):
                ket_piece(1, q, up_send, plane_at(1) * 2).start()
                ket_piece(1, q, down_send, plane_at(NZ - 1) * 2).start()
            start_bt()

        def send_part(p, i):
            return remote(
                part.at[p, i], got.at[p, i], part_send.at[p], part_recv.at[p], site, slot_at(PLANE[i])
            )

        def all_parts(p):
            span = pl.ds(0, N_PLANE)
            return remote(
                part.at[p, span], got.at[p, span], part_send.at[p], part_recv.at[p],
                site, slot_at(PLANE[0]),
            )

        def send_rows(q, d):
            held = env.at[q, rows]
            return remote(held, held, env_send.at[q], env_recv.at[q], plane_at(d) * 2 + 1)

        def all_rows(q):
            held = env.at[q, pl.ds(0, N_COLUMN * ROWS)]
            return remote(held, held, env_send.at[q], env_recv.at[q], plane_at(COLUMN[0]) * 2 + 1)

        def scatter(p):
            def summed(slot):
                return (prod[lookup[p, 0, slot]] + prod[lookup[p, 1, slot]]).astype(BF16)

            for i in range(N_PLANE):
                part[p, i] = summed(slot_at(PLANE[i]))
                send_part(p, i).start()
            got[p, N_PLANE] = summed(sector)

        def gather(p):
            all_parts(p).wait_recv()
            total = got[p, 0].astype(F32)
            for i in range(1, SLOTS):
                total += got[p, i].astype(F32)
            env[1 - p, rows] = total.astype(BF16)
            for d in COLUMN:
                send_rows(1 - p, d).start()

        def fetch(j, p):
            return pltpu.make_async_copy(tables.at[j], lookup.at[p], table_sem.at[p])

        def fetch_table(j, p):
            @pl.when(j != site)
            def _():
                remote(tables.at[j], tables.at[j], table_send, table_recv.at[j], z * 2).wait_recv()

            fetch(j, p).start()

        fetch_table(0, 0)
        remote(first_in, first_in, first_send, first_recv, z * 2).wait_recv()
        for k in range(TRIP):
            prod[k] = first_in[k * ROWS:(k + 1) * ROWS].astype(F32)
        fetch(0, 0).wait()
        scatter(0)
        fetch_table(1, 1)

        @pl.when(site == 3)
        def _():
            start_bt()

        gather(0)

        def step(j, carry):
            p = lax.rem(j, 2)

            @pl.when(j != site)
            def _():
                remote(bt.at[j], bt.at[j], bt_send, bt_recv.at[j], z * 2).wait_recv()
                whole_ket(j, over_send).wait_recv()

            all_rows(p).wait_recv()
            left = jnp.dot(bt[j], env[p], preferred_element_type=F32).astype(BF16)
            for k in range(TRIP):
                prod[k] = jnp.dot(
                    left[k * ROWS:(k + 1) * ROWS], kets[j, k], preferred_element_type=F32
                )
            fetch(j, p).wait()
            scatter(p)

            @pl.when(j < STEPS - 1)
            def _():
                fetch_table(j + 1, 1 - p)

            all_parts(1 - p).wait_send()
            all_rows(p).wait_send()

            @pl.when(j == z * 2)
            def _():
                leave[...] = env[p]
                to_core_0().start()

            @pl.when(j == site)
            def _():
                out_ref[...] = env[p]

            @pl.when((j == site - 3) & (site < STEPS))
            def _():
                start_bt()

            gather(p)
            return carry

        lax.fori_loop(1, STEPS, step, 0)
        last = STEPS % 2
        all_rows(last).wait_recv()

        @pl.when(site == STEPS)
        def _():
            out_ref[...] = env[last]

        all_rows(last).wait_send()
        all_parts(1 - last).wait_send()

        @pl.when(z > 0)
        def _():
            to_core_0().wait_send()

        @pl.when(site < STEPS)
        def _():
            for d in COLUMN:
                send_table(d).wait_send()
                send_bt(d).wait_send()

        @pl.when((site > 1) & (site < STEPS))
        def _():
            whole_ket(site, over_send).wait_send()

        @pl.when(site == 1)
        def _():
            whole_ket(1, up_send).wait_send()
            whole_ket(1, down_send).wait_send()


def run_chain(env, bra, ket, outputs, terms, owner, weight):
    vmem = pl.BlockSpec(memory_space=pltpu.VMEM)
    smem = pl.BlockSpec(memory_space=pltpu.SMEM)
    anywhere = pl.BlockSpec(memory_space=pl.ANY)
    dma = pltpu.SemaphoreType.DMA
    return pl.pallas_call(
        chain,
        out_shape=jax.ShapeDtypeStruct((TILE, TILE), BF16),
        in_specs=[vmem, anywhere, anywhere, smem, smem, smem, smem],
        out_specs=vmem,
        scratch_shapes=[
            pltpu.VMEM((TRIP, TILE, TILE), BF16),
            pltpu.VMEM((2, TILE, TILE), BF16),
            pltpu.VMEM((TRIP + 1, ROWS, TILE), F32),
            pltpu.VMEM((2, N_PLANE, ROWS, TILE), BF16),
            pltpu.VMEM((2, SLOTS, ROWS, TILE), BF16),
            pltpu.VMEM((TILE, TILE), BF16),
            pltpu.VMEM((TILE, TILE), BF16),
            pltpu.VMEM((NZ, TRIP * ROWS, TILE), BF16),
            pltpu.VMEM((2 * NZ, TRIP * ROWS, TILE), BF16),
            pltpu.VMEM((NZ, TRIP * ROWS, TILE), BF16),
            pltpu.VMEM((TRIP * ROWS, TILE), BF16),
            pltpu.VMEM((2 * NZ, TRIP, TILE, TILE), BF16),
            pltpu.VMEM((2 * NZ, 8, TILE), jnp.int32),
            pltpu.SMEM((2, 8, TILE), jnp.int32),
            dma((2,)), dma((2,)), dma((2,)), dma((2,)), dma, dma, dma, dma((2 * NZ,)),
            dma, dma, dma, dma((2 * NZ,)), dma((2,)), dma((2,)),
            dma, dma, dma, dma((2 * NZ, PIECES)),
        ],
        compiler_params=pltpu.CompilerParams(
            collective_id=0, has_side_effects=True, vmem_limit_bytes=56 << 20
        ),
        name="chain",
    )(env, bra, ket, outputs, terms, owner, weight)


def local(left_env, mps_bra, mps_ket, joining_out, joining_mpo, owner, mpo_weight):
    envs = run_chain(
        left_env[0], mps_bra[0], mps_ket[0], joining_out[0, :, 0], joining_mpo[0], owner, mpo_weight[0]
    )
    return envs[None, None]


def solution(mesh):
    return jax.shard_map(
        local,
        mesh=mesh,
        in_specs=(
            P("sector", None, None),
            P("site", "sector", None, None),
            P("site", "sector", None, None),
            P("site", "sector", None),
            P("site", "sector"),
            P(),
            P("site", None),
        ),
        out_specs=P("site", "sector", None, None),
        check_vma=False,
    )
```

```python
import functools

import jax
import jax.numpy as jnp
from jax import lax
from jax.experimental import pallas as pl
from jax.experimental.pallas import tpu as pltpu
from jax.sharding import PartitionSpec as P

MESH = pl.DeviceIdType.MESH
BF16 = jnp.bfloat16
F32 = jnp.float32

NX, NY, NZ = 4, 8, 8
SLOTS = NX * NY
STEPS = 15
TRIP = 16
ROWS = 16
TILE = 128
PIECES = 16
PIECE = TRIP // PIECES
LEAD = 8


def hops(offset):
    dy, dx = offset
    return min(dy, NY - dy) + min(dx, NX - dx)


PLANE = sorted(
    [(dy, dx) for dy in range(NY) for dx in range(NX) if (dy, dx) != (0, 0)], key=hops, reverse=True
)
COLUMN = sorted(range(1, NZ), key=lambda d: min(d, NZ - d), reverse=True)
N_PLANE = len(PLANE)
N_COLUMN = len(COLUMN)
N_FAR = sum(hops(offset) > 4 for offset in PLANE)


def chain(
    env_ref, bra_ref, ket_ref, outputs_ref, terms_ref, owner_ref, weight_ref, out_ref,
    bra, env, prod, part, got, leave, land, bt_out, bt, first_out, first_in, kets, tables, lookup,
    part_send, part_recv, env_send, env_recv, out_send, out_recv, bt_send, bt_recv,
    first_send, first_recv, table_send, table_recv, table_sem, local_sem,
    up_send, down_send, over_send, ket_recv, gate,
):
    site = lax.axis_index("site")
    sector = lax.axis_index("sector")
    z, core = site // 2, lax.rem(site, 2)
    y, x = sector // NX, lax.rem(sector, NX)
    rows = pl.ds(pl.multiple_of(z * ROWS, ROWS), ROWS)

    def slot_at(offset):
        return lax.rem(y + offset[0], NY) * NX + lax.rem(x + offset[1], NX)

    def plane_at(d):
        return lax.rem(z + d, NZ)

    def remote(src, dst, send_sem, recv_sem, to_site, to_sector=sector):
        return pltpu.make_async_remote_copy(
            src_ref=src, dst_ref=dst, send_sem=send_sem, recv_sem=recv_sem,
            device_id=(to_site, to_sector), device_id_type=MESH,
        )

    barrier = pltpu.get_barrier_semaphore()

    def greet(to_site, to_sector=sector):
        pl.semaphore_signal(barrier, inc=1, device_id=(to_site, to_sector), device_id_type=MESH)

    def send_table(d):
        return remote(tables.at[site], tables.at[site], table_send, table_recv.at[site], plane_at(d) * 2 + 1)

    def send_bt(d):
        return remote(
            bt_out.at[plane_at(d)], bt.at[site], bt_send, bt_recv.at[site], plane_at(d) * 2 + 1
        )

    def send_first(c, i):
        to_sector = sector if i == N_PLANE else slot_at(PLANE[i])
        return remote(first_out.at[c, i], first_in.at[c, i], first_send, first_recv.at[c], 1, to_sector)

    def to_core_0():
        return remote(leave, land, out_send, out_recv, z * 2)

    def ket_piece(f, q, send_sem, to_site):
        held = kets.at[f, pl.ds(q * PIECE, PIECE)]
        return remote(held, held, send_sem, ket_recv.at[f, q], to_site)

    def whole_ket(f, send_sem, tiles=TRIP):
        held = kets.at[f, pl.ds(0, tiles)]
        return remote(held, held, send_sem, ket_recv.at[f, 0], site + 1 - 2 * core)

    own_ket = pltpu.make_async_copy(ket_ref, kets.at[site], local_sem.at[0])
    own_bra = pltpu.make_async_copy(bra_ref, bra, local_sem.at[1])
    own_ket.start()
    own_bra.start()
    def fetch(j, p):
        return pltpu.make_async_copy(tables.at[j], lookup.at[p], table_sem.at[p])

    def products(bt_chunk, block, j):
        left = jnp.dot(bt_chunk, block, preferred_element_type=F32).astype(BF16)
        for k in range(TRIP):
            prod[k] = jnp.dot(
                left[k * ROWS:(k + 1) * ROWS], kets[j, k], preferred_element_type=F32
            )

    def summed(p, slot):
        return (prod[lookup[p, 0, slot]] + prod[lookup[p, 1, slot]]).astype(BF16)

    @pl.when(core == 0)
    def _():
        greet(plane_at(1) * 2)
        greet(plane_at(NZ - 1) * 2)

        @pl.when(z > 0)
        def _():
            greet(site + 1)

    @pl.when(core == 1)
    def _():
        for offset in PLANE:
            greet(site, slot_at(offset))

            @pl.when(z == 0)
            def _():
                greet(0, slot_at(offset))
        for d in COLUMN:
            greet(plane_at(d) * 2 + 1)
            greet(plane_at(d) * 2)
        greet(site - 1)

    lane = lax.broadcasted_iota(jnp.int32, (8, TILE), 1)
    first = jnp.full((8, TILE), TRIP, jnp.int32)
    second = first
    for k in reversed(range(TRIP)):
        hit = lane == owner_ref[outputs_ref[k]]
        second = jnp.where(hit, first, second)
        first = jnp.where(hit, k, first)
    upper = lax.broadcasted_iota(jnp.int32, (8, TILE), 0) == 0
    tables[site] = jnp.where(upper, first, second)

    own_bra.wait()
    for k in range(TRIP):
        turned = jnp.transpose(bra[k].astype(F32)) * weight_ref[terms_ref[k]]
        bt_out[:, k * ROWS:(k + 1) * ROWS, :] = turned.astype(BF16).reshape(NZ, ROWS, TILE)
    own_ket.wait()

    @pl.when(core == 0)
    def _():
        pl.semaphore_wait(barrier, N_COLUMN + 3 + jnp.where(z == 0, N_PLANE, 0))

        @pl.when(z == 0)
        def _():
            prod[TRIP] = jnp.zeros((ROWS, TILE), F32)
            fetch(0, 0).start()
            fetch(0, 0).wait()

            def chunk(c, carry):
                products(bt_out[c], env_ref[...], 0)
                for i in range(SLOTS):
                    first_out[c, i] = summed(0, sector if i == N_PLANE else slot_at(PLANE[i]))
                    send_first(c, i).start()
                return carry

            lax.fori_loop(0, NZ, chunk, 0)
            out_ref[...] = env_ref[...]

        @pl.when(z > 0)
        def _():
            for d in COLUMN + [0]:
                send_table(d).start()

        def send_own(up, down):
            for q in range(PIECES):
                if up:
                    ket_piece(site, q, up_send, plane_at(1) * 2).start()
                if down:
                    held = kets.at[site, pl.ds(q * PIECE, PIECE)]
                    ket_piece(site, q, down_send, plane_at(NZ - 1) * 2).start()
                    remote(held, held, over_send, ket_recv.at[site, 0], z * 2 + 1).start()

        @pl.when(z == 1)
        def _():
            send_own(False, True)

        @pl.when(z > 0)
        def _():
            pl.semaphore_wait(gate, 1)

        @pl.when(z == 1)
        def _():
            send_own(True, False)

        @pl.when(z > 0)
        def _():
            for d in COLUMN + [0]:
                send_bt(d).start()

        def serve(f, carry):
            away = lax.rem(z - f // 2 + NZ, NZ)


            @pl.when(f != site)
            def _():
                for q in range(PIECES):
                    ket_piece(f, q, up_send, z * 2 + 1).wait_recv()
                    if 2 * q < PIECES:
                        up, down = away < NZ // 2, (away == 0) | (away > NZ // 2 + 1)
                    else:
                        up, down = away < NZ // 2 - 1, (away == 0) | (away > NZ // 2)
                    held = kets.at[f, pl.ds(q * PIECE, PIECE)]

                    @pl.when(up)
                    def _():
                        ket_piece(f, q, up_send, plane_at(1) * 2).start()

                    @pl.when(down)
                    def _():
                        ket_piece(f, q, down_send, plane_at(NZ - 1) * 2).start()

                    @pl.when(away > 0)
                    def _():
                        remote(held, held, over_send, ket_recv.at[f, 0], z * 2 + 1).start()

            @pl.when((f == jnp.minimum(site - 1, LEAD)) & (z > 1))
            def _():
                send_own(True, True)

            return carry

        lax.fori_loop(2, STEPS, serve, 0)

        @pl.when(z > 0)
        def _():
            to_core_0().wait_recv()
            out_ref[...] = land[...]

        def settle(f, carry):
            away = lax.rem(z - f // 2 + NZ, NZ)

            @pl.when(away < NZ // 2 - 1)
            def _():
                whole_ket(f, up_send).wait_send()

            @pl.when(away == NZ // 2 - 1)
            def _():
                whole_ket(f, up_send, TRIP // 2).wait_send()

            @pl.when((away == 0) | (away > NZ // 2 + 1))
            def _():
                whole_ket(f, down_send).wait_send()

            @pl.when(away == NZ // 2 + 1)
            def _():
                whole_ket(f, down_send, TRIP // 2).wait_send()

            @pl.when((away > 0) | (f == site))
            def _():
                whole_ket(f, over_send).wait_send()

            return carry

        lax.fori_loop(2, STEPS, settle, 0)
        @pl.when(z == 0)
        def _():
            remote(first_out, first_in, first_send, first_recv.at[0], 1).wait_send()

        @pl.when(z > 0)
        def _():
            for d in COLUMN + [0]:
                send_table(d).wait_send()
                send_bt(d).wait_send()

    @pl.when(core == 1)
    def _():
        prod[TRIP] = jnp.zeros((ROWS, TILE), F32)
        bt[site] = bt_out[z]
        pl.semaphore_wait(barrier, N_PLANE + N_COLUMN + jnp.where(z == 0, 0, 1))
        @pl.when(site < STEPS)
        def _():
            for d in COLUMN:
                send_table(d).start()

        @pl.when((site > 1) & (site < STEPS))
        def _():
            for q in range(PIECES):
                ket_piece(site, q, over_send, z * 2).start()

        def start_bt():
            for d in COLUMN:
                send_bt(d).start()

        half = PIECES // 2

        def first_kets(pieces, up, down, source=False):
            for q in pieces:
                for way, sem, d in ((up, up_send, 1), (down, down_send, NZ - 1)):
                    @pl.when(way)
                    def _():
                        if not source:
                            ket_piece(1, q, sem, site).wait_recv()
                        ket_piece(1, q, sem, plane_at(d) * 2 + 1).start()

        def take_kets(pieces):
            for q in pieces:
                ket_piece(1, q, up_send, site).wait_recv()

        first_kets(range(PIECES), z == 0, z == 0, source=True)

        @pl.when(site == 1)
        def _():
            start_bt()

        next_up, next_down = (z == 1) | (z == 2), (z == NZ - 1) | (z == NZ - 2)
        first_kets(range(half), next_up | (z == 3), next_down)
        first_kets(range(half, PIECES), next_up, next_down | (z == NZ - 3))

        @pl.when(z > 0)
        def _():
            pl.semaphore_signal(gate, inc=1, device_id=(z * 2, sector), device_id_type=MESH)

        @pl.when((z == 4) | (z == 5))
        def _():
            take_kets(range(half))

        @pl.when((z == 3) | (z == 4))
        def _():
            take_kets(range(half, PIECES))

        def send_part(p, i):
            return remote(
                part.at[p, i], got.at[p, i], part_send.at[p], part_recv.at[p, int(i >= N_FAR)],
                site, slot_at(PLANE[i]),
            )

        def some_parts(p, start, count, group=0):
            span = pl.ds(start, count)
            return remote(
                part.at[p, span], got.at[p, span], part_send.at[p], part_recv.at[p, group],
                site, slot_at(PLANE[0]),
            )

        def send_rows(q, d):
            held = env.at[q, rows]
            return remote(held, held, env_send.at[q], env_recv.at[q], plane_at(d) * 2 + 1)

        def all_rows(q):
            held = env.at[q, pl.ds(0, N_COLUMN * ROWS)]
            return remote(held, held, env_send.at[q], env_recv.at[q], plane_at(COLUMN[0]) * 2 + 1)

        def scatter(p):
            for i in range(N_PLANE):
                part[p, i] = summed(p, slot_at(PLANE[i]))
                send_part(p, i).start()
            got[p, N_PLANE] = summed(p, sector)

        def gather(p):
            some_parts(p, N_FAR, N_PLANE - N_FAR, 1).wait_recv()
            total = got[p, N_FAR].astype(F32)
            for i in range(N_FAR + 1, SLOTS):
                total += got[p, i].astype(F32)
            some_parts(p, 0, N_FAR).wait_recv()
            for i in range(N_FAR):
                total += got[p, i].astype(F32)
            env[1 - p, rows] = total.astype(BF16)
            for d in COLUMN:
                send_rows(1 - p, d).start()

        def fetch_table(j, p):
            @pl.when(j != site)
            def _():
                remote(tables.at[j], tables.at[j], table_send, table_recv.at[j], z * 2).wait_recv()

            fetch(j, p).start()

        fetch_table(1, 1)

        @pl.when(z == 0)
        def _():
            def chunk(c, carry):
                remote(first_in.at[c], first_in.at[c], first_send, first_recv.at[c], 0).wait_recv()
                total = first_in[c, 0].astype(F32)
                for i in range(1, SLOTS):
                    total += first_in[c, i].astype(F32)
                part_rows = pl.ds(pl.multiple_of(c * ROWS, ROWS), ROWS)
                env[1, part_rows] = total.astype(BF16)
                for d in COLUMN:
                    held = env.at[1, part_rows]
                    remote(held, held, env_send.at[1], env_recv.at[1], plane_at(d) * 2 + 1).start()
                return carry

            lax.fori_loop(0, NZ, chunk, 0)

        def whole_env(q):
            return remote(env.at[q], env.at[q], env_send.at[q], env_recv.at[q], plane_at(1) * 2 + 1)

        @pl.when(z > 0)
        def _():
            whole_env(1).wait_recv()

        def step(j, carry):
            p = lax.rem(j, 2)

            @pl.when(j != site)
            def _():
                remote(bt.at[j], bt.at[j], bt_send, bt_recv.at[j], z * 2).wait_recv()

                @pl.when(j > 1)
                def _():
                    whole_ket(j, over_send).wait_recv()

            @pl.when(j > 1)
            def _():
                all_rows(p).wait_recv()

            products(bt[j], env[p], j)
            fetch(j, p).wait()
            scatter(p)

            @pl.when(j < STEPS - 1)
            def _():
                fetch_table(j + 1, 1 - p)

            @pl.when(j > 1)
            def _():
                some_parts(1 - p, 0, N_PLANE).wait_send()
                all_rows(p).wait_send()

            @pl.when((j == 1) & (z == 0))
            def _():
                for d in COLUMN:
                    whole_env(1).wait_send()

            @pl.when(j == z * 2)
            def _():
                leave[...] = env[p]
                to_core_0().start()

            @pl.when(j == site)
            def _():
                out_ref[...] = env[p]

            @pl.when((j == jnp.maximum(site - 3, 1)) & (site > 1) & (site < STEPS))
            def _():
                start_bt()

            gather(p)
            return carry

        lax.fori_loop(1, STEPS, step, 0)
        last = STEPS % 2
        all_rows(last).wait_recv()

        @pl.when(site == STEPS)
        def _():
            out_ref[...] = env[last]

        all_rows(last).wait_send()
        some_parts(1 - last, 0, N_PLANE).wait_send()

        @pl.when(z > 0)
        def _():
            to_core_0().wait_send()

        @pl.when(site < STEPS)
        def _():
            for d in COLUMN:
                send_table(d).wait_send()
                send_bt(d).wait_send()

        @pl.when((site > 1) & (site < STEPS))
        def _():
            whole_ket(site, over_send).wait_send()

        @pl.when(z < 3)
        def _():
            whole_ket(1, up_send).wait_send()

        @pl.when(z == 3)
        def _():
            whole_ket(1, up_send, TRIP // 2).wait_send()

        @pl.when((z == 0) | (z > 5))
        def _():
            whole_ket(1, down_send).wait_send()

        @pl.when(z == 5)
        def _():
            whole_ket(1, down_send, TRIP // 2).wait_send()


def run_chain(env, bra, ket, outputs, terms, owner, weight):
    vmem = pl.BlockSpec(memory_space=pltpu.VMEM)
    smem = pl.BlockSpec(memory_space=pltpu.SMEM)
    anywhere = pl.BlockSpec(memory_space=pl.ANY)
    dma = pltpu.SemaphoreType.DMA
    return pl.pallas_call(
        chain,
        out_shape=jax.ShapeDtypeStruct((TILE, TILE), BF16),
        in_specs=[vmem, anywhere, anywhere, smem, smem, smem, smem],
        out_specs=vmem,
        scratch_shapes=[
            pltpu.VMEM((TRIP, TILE, TILE), BF16),
            pltpu.VMEM((2, TILE, TILE), BF16),
            pltpu.VMEM((TRIP + 1, ROWS, TILE), F32),
            pltpu.VMEM((2, N_PLANE, ROWS, TILE), BF16),
            pltpu.VMEM((2, SLOTS, ROWS, TILE), BF16),
            pltpu.VMEM((TILE, TILE), BF16),
            pltpu.VMEM((TILE, TILE), BF16),
            pltpu.VMEM((NZ, TRIP * ROWS, TILE), BF16),
            pltpu.VMEM((2 * NZ, TRIP * ROWS, TILE), BF16),
            pltpu.VMEM((NZ, SLOTS, ROWS, TILE), BF16),
            pltpu.VMEM((NZ, SLOTS, ROWS, TILE), BF16),
            pltpu.VMEM((2 * NZ, TRIP, TILE, TILE), BF16),
            pltpu.VMEM((2 * NZ, 8, TILE), jnp.int32),
            pltpu.SMEM((2, 8, TILE), jnp.int32),
            dma((2,)), dma((2, 2)), dma((2,)), dma((2,)), dma, dma, dma, dma((2 * NZ,)),
            dma, dma((NZ,)), dma, dma((2 * NZ,)), dma((2,)), dma((2,)),
            dma, dma, dma, dma((2 * NZ, PIECES)),
            pltpu.SemaphoreType.REGULAR,
        ],
        compiler_params=pltpu.CompilerParams(
            collective_id=0, has_side_effects=True, vmem_limit_bytes=56 << 20
        ),
        name="chain",
    )(env, bra, ket, outputs, terms, owner, weight)


def local(left_env, mps_bra, mps_ket, joining_out, joining_mpo, owner, mpo_weight):
    envs = run_chain(
        left_env[0], mps_bra[0], mps_ket[0], joining_out[0, :, 0], joining_mpo[0], owner, mpo_weight[0]
    )
    return envs[None, None]


def solution(mesh):
    return jax.shard_map(
        local,
        mesh=mesh,
        in_specs=(
            P("sector", None, None),
            P("site", "sector", None, None),
            P("site", "sector", None, None),
            P("site", "sector", None),
            P("site", "sector"),
            P(),
            P("site", None),
        ),
        out_specs=P("site", "sector", None, None),
        check_vma=False,
    )
```

```python
import functools

import jax
import jax.numpy as jnp
from jax import lax
from jax.experimental import pallas as pl
from jax.experimental.pallas import tpu as pltpu
from jax.sharding import PartitionSpec as P

MESH = pl.DeviceIdType.MESH
BF16 = jnp.bfloat16
F32 = jnp.float32

NX, NY, NZ = 4, 8, 8
SLOTS = NX * NY
STEPS = 15
TRIP = 16
ROWS = 16
TILE = 128
PIECES = 16
PIECE = TRIP // PIECES
LEAD = 8


def hops(offset):
    dy, dx = offset
    return min(dy, NY - dy) + min(dx, NX - dx)


PLANE = sorted(
    [(dy, dx) for dy in range(NY) for dx in range(NX) if (dy, dx) != (0, 0)], key=hops, reverse=True
)
COLUMN = sorted(range(1, NZ), key=lambda d: min(d, NZ - d), reverse=True)
N_PLANE = len(PLANE)
N_COLUMN = len(COLUMN)
N_FAR = sum(hops(offset) > 4 for offset in PLANE)


def chain(
    env_ref, bra_ref, ket_ref, outputs_ref, terms_ref, owner_ref, weight_ref, out_ref,
    bra, env, prod, part, got, leave, land, bt_out, bt, first_out, first_in, kets, tables, lookup,
    part_send, part_recv, env_send, env_recv, out_send, out_recv, bt_send, bt_recv,
    first_send, first_recv, table_send, table_recv, table_sem, local_sem,
    up_send, down_send, over_send, ket_recv, gate,
):
    site = lax.axis_index("site")
    sector = lax.axis_index("sector")
    z, core = site // 2, lax.rem(site, 2)
    y, x = sector // NX, lax.rem(sector, NX)
    rows = pl.ds(pl.multiple_of(z * ROWS, ROWS), ROWS)

    def slot_at(offset):
        return lax.rem(y + offset[0], NY) * NX + lax.rem(x + offset[1], NX)

    def plane_at(d):
        return lax.rem(z + d, NZ)

    def remote(src, dst, send_sem, recv_sem, to_site, to_sector=sector):
        return pltpu.make_async_remote_copy(
            src_ref=src, dst_ref=dst, send_sem=send_sem, recv_sem=recv_sem,
            device_id=(to_site, to_sector), device_id_type=MESH,
        )

    barrier = pltpu.get_barrier_semaphore()

    def greet(to_site, to_sector=sector):
        pl.semaphore_signal(barrier, inc=1, device_id=(to_site, to_sector), device_id_type=MESH)

    def send_table(d):
        return remote(tables.at[site], tables.at[site], table_send, table_recv.at[site], plane_at(d) * 2 + 1)

    def send_bt(d):
        return remote(
            bt_out.at[plane_at(d)], bt.at[site], bt_send, bt_recv.at[site], plane_at(d) * 2 + 1
        )

    def send_first(c, i):
        to_sector = sector if i == N_PLANE else slot_at(PLANE[i])
        return remote(first_out.at[c, i], first_in.at[c, i], first_send, first_recv.at[c], 1, to_sector)

    def to_core_0():
        return remote(leave, land, out_send, out_recv, z * 2)

    def ket_piece(f, q, send_sem, to_site):
        held = kets.at[f, pl.ds(q * PIECE, PIECE)]
        return remote(held, held, send_sem, ket_recv.at[f, q], to_site)

    def whole_ket(f, send_sem, tiles=TRIP):
        held = kets.at[f, pl.ds(0, tiles)]
        return remote(held, held, send_sem, ket_recv.at[f, 0], site + 1 - 2 * core)

    own_ket = pltpu.make_async_copy(ket_ref, kets.at[site], local_sem.at[0])
    own_bra = pltpu.make_async_copy(bra_ref, bra, local_sem.at[1])
    own_ket.start()
    own_bra.start()
    def fetch(j, p):
        return pltpu.make_async_copy(tables.at[j], lookup.at[p], table_sem.at[p])

    def products(bt_chunk, block, j):
        left = jnp.dot(bt_chunk, block, preferred_element_type=F32).astype(BF16)
        for k in range(0, TRIP, 2):
            pair = jnp.concatenate([kets[j, k], kets[j, k + 1]], axis=1)
            both = jnp.dot(left[k * ROWS:(k + 2) * ROWS], pair, preferred_element_type=F32)
            prod[k] = both[:ROWS, :TILE]
            prod[k + 1] = both[ROWS:, TILE:]

    def summed(p, slot):
        return (prod[lookup[p, 0, slot]] + prod[lookup[p, 1, slot]]).astype(BF16)

    @pl.when(core == 0)
    def _():
        greet(plane_at(1) * 2)
        greet(plane_at(NZ - 1) * 2)

        @pl.when(z > 0)
        def _():
            greet(site + 1)

    @pl.when(core == 1)
    def _():
        for offset in PLANE:
            greet(site, slot_at(offset))

            @pl.when(z == 0)
            def _():
                greet(0, slot_at(offset))
        for d in COLUMN:
            greet(plane_at(d) * 2 + 1)
            greet(plane_at(d) * 2)
        greet(site - 1)

    lane = lax.broadcasted_iota(jnp.int32, (8, TILE), 1)
    first = jnp.full((8, TILE), TRIP, jnp.int32)
    second = first
    for k in reversed(range(TRIP)):
        hit = lane == owner_ref[outputs_ref[k]]
        second = jnp.where(hit, first, second)
        first = jnp.where(hit, k, first)
    upper = lax.broadcasted_iota(jnp.int32, (8, TILE), 0) == 0
    tables[site] = jnp.where(upper, first, second)

    own_bra.wait()
    for k in range(TRIP):
        turned = jnp.transpose(bra[k].astype(F32)) * weight_ref[terms_ref[k]]
        bt_out[:, k * ROWS:(k + 1) * ROWS, :] = turned.astype(BF16).reshape(NZ, ROWS, TILE)
    own_ket.wait()

    @pl.when(core == 0)
    def _():
        pl.semaphore_wait(barrier, N_COLUMN + 3 + jnp.where(z == 0, N_PLANE, 0))

        @pl.when(z == 0)
        def _():
            prod[TRIP] = jnp.zeros((ROWS, TILE), F32)
            fetch(0, 0).start()
            fetch(0, 0).wait()

            def chunk(c, carry):
                products(bt_out[c], env_ref[...], 0)
                for i in range(SLOTS):
                    first_out[c, i] = summed(0, sector if i == N_PLANE else slot_at(PLANE[i]))
                    send_first(c, i).start()
                return carry

            lax.fori_loop(0, NZ, chunk, 0)
            out_ref[...] = env_ref[...]

        @pl.when(z > 0)
        def _():
            for d in COLUMN + [0]:
                send_table(d).start()

        def send_own(up, down):
            for q in range(PIECES):
                if up:
                    ket_piece(site, q, up_send, plane_at(1) * 2).start()
                if down:
                    held = kets.at[site, pl.ds(q * PIECE, PIECE)]
                    ket_piece(site, q, down_send, plane_at(NZ - 1) * 2).start()
                    remote(held, held, over_send, ket_recv.at[site, 0], z * 2 + 1).start()

        @pl.when(z == 1)
        def _():
            send_own(False, True)

        @pl.when(z > 0)
        def _():
            pl.semaphore_wait(gate, 1)

        @pl.when(z == 1)
        def _():
            send_own(True, False)

        @pl.when(z > 0)
        def _():
            for d in COLUMN + [0]:
                send_bt(d).start()

        def serve(f, carry):
            away = lax.rem(z - f // 2 + NZ, NZ)


            @pl.when(f != site)
            def _():
                for q in range(PIECES):
                    ket_piece(f, q, up_send, z * 2 + 1).wait_recv()
                    if 2 * q < PIECES:
                        up, down = away < NZ // 2, (away == 0) | (away > NZ // 2 + 1)
                    else:
                        up, down = away < NZ // 2 - 1, (away == 0) | (away > NZ // 2)
                    held = kets.at[f, pl.ds(q * PIECE, PIECE)]

                    @pl.when(up)
                    def _():
                        ket_piece(f, q, up_send, plane_at(1) * 2).start()

                    @pl.when(down)
                    def _():
                        ket_piece(f, q, down_send, plane_at(NZ - 1) * 2).start()

                    @pl.when(away > 0)
                    def _():
                        remote(held, held, over_send, ket_recv.at[f, 0], z * 2 + 1).start()

            @pl.when((f == jnp.minimum(site - 1, LEAD)) & (z > 1))
            def _():
                send_own(True, True)

            return carry

        lax.fori_loop(2, STEPS, serve, 0)

        @pl.when(z > 0)
        def _():
            to_core_0().wait_recv()
            out_ref[...] = land[...]

        def settle(f, carry):
            away = lax.rem(z - f // 2 + NZ, NZ)

            @pl.when(away < NZ // 2 - 1)
            def _():
                whole_ket(f, up_send).wait_send()

            @pl.when(away == NZ // 2 - 1)
            def _():
                whole_ket(f, up_send, TRIP // 2).wait_send()

            @pl.when((away == 0) | (away > NZ // 2 + 1))
            def _():
                whole_ket(f, down_send).wait_send()

            @pl.when(away == NZ // 2 + 1)
            def _():
                whole_ket(f, down_send, TRIP // 2).wait_send()

            @pl.when((away > 0) | (f == site))
            def _():
                whole_ket(f, over_send).wait_send()

            return carry

        lax.fori_loop(2, STEPS, settle, 0)
        @pl.when(z == 0)
        def _():
            remote(first_out, first_in, first_send, first_recv.at[0], 1).wait_send()

        @pl.when(z > 0)
        def _():
            for d in COLUMN + [0]:
                send_table(d).wait_send()
                send_bt(d).wait_send()

    @pl.when(core == 1)
    def _():
        prod[TRIP] = jnp.zeros((ROWS, TILE), F32)
        bt[site] = bt_out[z]
        pl.semaphore_wait(barrier, N_PLANE + N_COLUMN + jnp.where(z == 0, 0, 1))
        @pl.when(site < STEPS)
        def _():
            for d in COLUMN:
                send_table(d).start()

        @pl.when((site > 1) & (site < STEPS))
        def _():
            for q in range(PIECES):
                ket_piece(site, q, over_send, z * 2).start()

        def start_bt():
            for d in COLUMN:
                send_bt(d).start()

        half = PIECES // 2

        def first_kets(pieces, up, down, source=False):
            for q in pieces:
                for way, sem, d in ((up, up_send, 1), (down, down_send, NZ - 1)):
                    @pl.when(way)
                    def _():
                        if not source:
                            ket_piece(1, q, sem, site).wait_recv()
                        ket_piece(1, q, sem, plane_at(d) * 2 + 1).start()

        def take_kets(pieces):
            for q in pieces:
                ket_piece(1, q, up_send, site).wait_recv()

        first_kets(range(PIECES), z == 0, z == 0, source=True)

        @pl.when(site == 1)
        def _():
            start_bt()

        next_up, next_down = (z == 1) | (z == 2), (z == NZ - 1) | (z == NZ - 2)
        first_kets(range(half), next_up | (z == 3), next_down)
        first_kets(range(half, PIECES), next_up, next_down | (z == NZ - 3))

        @pl.when(z > 0)
        def _():
            pl.semaphore_signal(gate, inc=1, device_id=(z * 2, sector), device_id_type=MESH)

        @pl.when((z == 4) | (z == 5))
        def _():
            take_kets(range(half))

        @pl.when((z == 3) | (z == 4))
        def _():
            take_kets(range(half, PIECES))

        def send_part(p, i):
            return remote(
                part.at[p, i], got.at[p, i], part_send.at[p], part_recv.at[p, int(i >= N_FAR)],
                site, slot_at(PLANE[i]),
            )

        def some_parts(p, start, count, group=0):
            span = pl.ds(start, count)
            return remote(
                part.at[p, span], got.at[p, span], part_send.at[p], part_recv.at[p, group],
                site, slot_at(PLANE[0]),
            )

        def send_rows(q, d):
            held = env.at[q, rows]
            return remote(held, held, env_send.at[q], env_recv.at[q], plane_at(d) * 2 + 1)

        def all_rows(q):
            held = env.at[q, pl.ds(0, N_COLUMN * ROWS)]
            return remote(held, held, env_send.at[q], env_recv.at[q], plane_at(COLUMN[0]) * 2 + 1)

        def scatter(p):
            for i in range(N_PLANE):
                part[p, i] = summed(p, slot_at(PLANE[i]))
                send_part(p, i).start()
            got[p, N_PLANE] = summed(p, sector)

        def gather(p):
            some_parts(p, N_FAR, N_PLANE - N_FAR, 1).wait_recv()
            total = got[p, N_FAR].astype(F32)
            for i in range(N_FAR + 1, SLOTS):
                total += got[p, i].astype(F32)
            some_parts(p, 0, N_FAR).wait_recv()
            for i in range(N_FAR):
                total += got[p, i].astype(F32)
            env[1 - p, rows] = total.astype(BF16)
            for d in COLUMN:
                send_rows(1 - p, d).start()

        def fetch_table(j, p):
            @pl.when(j != site)
            def _():
                remote(tables.at[j], tables.at[j], table_send, table_recv.at[j], z * 2).wait_recv()

            fetch(j, p).start()

        fetch_table(1, 1)

        @pl.when(z == 0)
        def _():
            def chunk(c, carry):
                remote(first_in.at[c], first_in.at[c], first_send, first_recv.at[c], 0).wait_recv()
                total = first_in[c, 0].astype(F32)
                for i in range(1, SLOTS):
                    total += first_in[c, i].astype(F32)
                part_rows = pl.ds(pl.multiple_of(c * ROWS, ROWS), ROWS)
                env[1, part_rows] = total.astype(BF16)
                for d in COLUMN:
                    held = env.at[1, part_rows]
                    remote(held, held, env_send.at[1], env_recv.at[1], plane_at(d) * 2 + 1).start()
                return carry

            lax.fori_loop(0, NZ, chunk, 0)

        def whole_env(q):
            return remote(env.at[q], env.at[q], env_send.at[q], env_recv.at[q], plane_at(1) * 2 + 1)

        @pl.when(z > 0)
        def _():
            whole_env(1).wait_recv()

        def step(j, carry):
            p = lax.rem(j, 2)

            @pl.when(j != site)
            def _():
                remote(bt.at[j], bt.at[j], bt_send, bt_recv.at[j], z * 2).wait_recv()

                @pl.when(j > 1)
                def _():
                    whole_ket(j, over_send).wait_recv()

            @pl.when(j > 1)
            def _():
                all_rows(p).wait_recv()

            products(bt[j], env[p], j)
            fetch(j, p).wait()
            scatter(p)

            @pl.when(j < STEPS - 1)
            def _():
                fetch_table(j + 1, 1 - p)

            @pl.when(j > 1)
            def _():
                some_parts(1 - p, 0, N_PLANE).wait_send()
                all_rows(p).wait_send()

            @pl.when((j == 1) & (z == 0))
            def _():
                for d in COLUMN:
                    whole_env(1).wait_send()

            @pl.when(j == z * 2)
            def _():
                leave[...] = env[p]
                to_core_0().start()

            @pl.when(j == site)
            def _():
                out_ref[...] = env[p]

            @pl.when((j == jnp.maximum(site - 2, 1)) & (site > 1) & (site < STEPS))
            def _():
                start_bt()

            gather(p)
            return carry

        lax.fori_loop(1, STEPS, step, 0)
        last = STEPS % 2
        all_rows(last).wait_recv()

        @pl.when(site == STEPS)
        def _():
            out_ref[...] = env[last]

        all_rows(last).wait_send()
        some_parts(1 - last, 0, N_PLANE).wait_send()

        @pl.when(z > 0)
        def _():
            to_core_0().wait_send()

        @pl.when(site < STEPS)
        def _():
            for d in COLUMN:
                send_table(d).wait_send()
                send_bt(d).wait_send()

        @pl.when((site > 1) & (site < STEPS))
        def _():
            whole_ket(site, over_send).wait_send()

        @pl.when(z < 3)
        def _():
            whole_ket(1, up_send).wait_send()

        @pl.when(z == 3)
        def _():
            whole_ket(1, up_send, TRIP // 2).wait_send()

        @pl.when((z == 0) | (z > 5))
        def _():
            whole_ket(1, down_send).wait_send()

        @pl.when(z == 5)
        def _():
            whole_ket(1, down_send, TRIP // 2).wait_send()


def run_chain(env, bra, ket, outputs, terms, owner, weight):
    vmem = pl.BlockSpec(memory_space=pltpu.VMEM)
    smem = pl.BlockSpec(memory_space=pltpu.SMEM)
    anywhere = pl.BlockSpec(memory_space=pl.ANY)
    dma = pltpu.SemaphoreType.DMA
    return pl.pallas_call(
        chain,
        out_shape=jax.ShapeDtypeStruct((TILE, TILE), BF16),
        in_specs=[vmem, anywhere, anywhere, smem, smem, smem, smem],
        out_specs=vmem,
        scratch_shapes=[
            pltpu.VMEM((TRIP, TILE, TILE), BF16),
            pltpu.VMEM((2, TILE, TILE), BF16),
            pltpu.VMEM((TRIP + 1, ROWS, TILE), F32),
            pltpu.VMEM((2, N_PLANE, ROWS, TILE), BF16),
            pltpu.VMEM((2, SLOTS, ROWS, TILE), BF16),
            pltpu.VMEM((TILE, TILE), BF16),
            pltpu.VMEM((TILE, TILE), BF16),
            pltpu.VMEM((NZ, TRIP * ROWS, TILE), BF16),
            pltpu.VMEM((2 * NZ, TRIP * ROWS, TILE), BF16),
            pltpu.VMEM((NZ, SLOTS, ROWS, TILE), BF16),
            pltpu.VMEM((NZ, SLOTS, ROWS, TILE), BF16),
            pltpu.VMEM((2 * NZ, TRIP, TILE, TILE), BF16),
            pltpu.VMEM((2 * NZ, 8, TILE), jnp.int32),
            pltpu.SMEM((2, 8, TILE), jnp.int32),
            dma((2,)), dma((2, 2)), dma((2,)), dma((2,)), dma, dma, dma, dma((2 * NZ,)),
            dma, dma((NZ,)), dma, dma((2 * NZ,)), dma((2,)), dma((2,)),
            dma, dma, dma, dma((2 * NZ, PIECES)),
            pltpu.SemaphoreType.REGULAR,
        ],
        compiler_params=pltpu.CompilerParams(
            collective_id=0, has_side_effects=True, vmem_limit_bytes=56 << 20
        ),
        name="chain",
    )(env, bra, ket, outputs, terms, owner, weight)


def local(left_env, mps_bra, mps_ket, joining_out, joining_mpo, owner, mpo_weight):
    envs = run_chain(
        left_env[0], mps_bra[0], mps_ket[0], joining_out[0, :, 0], joining_mpo[0], owner, mpo_weight[0]
    )
    return envs[None, None]


def solution(mesh):
    return jax.shard_map(
        local,
        mesh=mesh,
        in_specs=(
            P("sector", None, None),
            P("site", "sector", None, None),
            P("site", "sector", None, None),
            P("site", "sector", None),
            P("site", "sector"),
            P(),
            P("site", None),
        ),
        out_specs=P("site", "sector", None, None),
        check_vma=False,
    )
```

```python
import functools

import jax
import jax.numpy as jnp
from jax import lax
from jax.experimental import pallas as pl
from jax.experimental.pallas import tpu as pltpu
from jax.sharding import PartitionSpec as P

MESH = pl.DeviceIdType.MESH
BF16 = jnp.bfloat16
F32 = jnp.float32

NX, NY, NZ = 4, 8, 8
SLOTS = NX * NY
STEPS = 15
TRIP = 16
ROWS = 16
TILE = 128
PIECES = 16
PIECE = TRIP // PIECES
LEAD = 8
WIDE = 2


def hops(offset):
    dy, dx = offset
    return min(dy, NY - dy) + min(dx, NX - dx)


PLANE = sorted(
    [(dy, dx) for dy in range(NY) for dx in range(NX) if (dy, dx) != (0, 0)], key=hops, reverse=True
)
COLUMN = sorted(range(1, NZ), key=lambda d: min(d, NZ - d), reverse=True)
N_PLANE = len(PLANE)
N_COLUMN = len(COLUMN)
N_FAR = sum(hops(offset) > 4 for offset in PLANE)


def chain(
    env_ref, bra_ref, ket_ref, outputs_ref, terms_ref, owner_ref, weight_ref, out_ref,
    bra, env, prod, part, got, leave, land, bt_out, bt, first_out, first_in, kets, tables, lookup,
    part_send, part_recv, env_send, env_recv, out_send, out_recv, bt_send, bt_recv,
    first_send, first_recv, table_send, table_recv, table_sem, local_sem,
    up_send, down_send, over_send, ket_recv, gate,
):
    site = lax.axis_index("site")
    sector = lax.axis_index("sector")
    z, core = site // 2, lax.rem(site, 2)
    y, x = sector // NX, lax.rem(sector, NX)
    rows = pl.ds(pl.multiple_of(z * ROWS, ROWS), ROWS)

    def slot_at(offset):
        return lax.rem(y + offset[0], NY) * NX + lax.rem(x + offset[1], NX)

    def plane_at(d):
        return lax.rem(z + d, NZ)

    def remote(src, dst, send_sem, recv_sem, to_site, to_sector=sector):
        return pltpu.make_async_remote_copy(
            src_ref=src, dst_ref=dst, send_sem=send_sem, recv_sem=recv_sem,
            device_id=(to_site, to_sector), device_id_type=MESH,
        )

    barrier = pltpu.get_barrier_semaphore()

    def greet(to_site, to_sector=sector):
        pl.semaphore_signal(barrier, inc=1, device_id=(to_site, to_sector), device_id_type=MESH)

    def send_table(d):
        return remote(tables.at[site], tables.at[site], table_send, table_recv.at[site], plane_at(d) * 2 + 1)

    def send_bt(d):
        return remote(
            bt_out.at[plane_at(d)], bt.at[site], bt_send, bt_recv.at[site], plane_at(d) * 2 + 1
        )

    def send_first(c, i):
        to_sector = sector if i == N_PLANE else slot_at(PLANE[i])
        return remote(first_out.at[c, i], first_in.at[c, i], first_send, first_recv.at[c], 1, to_sector)

    def to_core_0():
        return remote(leave, land, out_send, out_recv, z * 2)

    def ket_piece(f, q, send_sem, to_site):
        held = kets.at[f, pl.ds(q * PIECE, PIECE)]
        return remote(held, held, send_sem, ket_recv.at[f, q], to_site)

    def whole_ket(f, send_sem, tiles=TRIP):
        held = kets.at[f, pl.ds(0, tiles)]
        return remote(held, held, send_sem, ket_recv.at[f, 0], site + 1 - 2 * core)

    own_ket = pltpu.make_async_copy(ket_ref, kets.at[site], local_sem.at[0])
    own_bra = pltpu.make_async_copy(bra_ref, bra, local_sem.at[1])
    own_ket.start()
    own_bra.start()
    def fetch(j, p):
        return pltpu.make_async_copy(tables.at[j], lookup.at[p], table_sem.at[p])

    def products(bt_chunk, block, j):
        left = jnp.dot(bt_chunk, block, preferred_element_type=F32).astype(BF16)
        for k in range(0, TRIP, 2):
            pair = jnp.concatenate([kets[j, k], kets[j, k + 1]], axis=1)
            both = jnp.dot(left[k * ROWS:(k + 2) * ROWS], pair, preferred_element_type=F32)
            prod[k] = both[:ROWS, :TILE]
            prod[k + 1] = both[ROWS:, TILE:]

    def summed(p, slot):
        return (prod[lookup[p, 0, slot]] + prod[lookup[p, 1, slot]]).astype(BF16)

    @pl.when(core == 0)
    def _():
        greet(plane_at(1) * 2)
        greet(plane_at(NZ - 1) * 2)

        @pl.when(z > 0)
        def _():
            greet(site + 1)

    @pl.when(core == 1)
    def _():
        for offset in PLANE:
            greet(site, slot_at(offset))

            @pl.when(z == 0)
            def _():
                greet(0, slot_at(offset))
        for d in COLUMN:
            greet(plane_at(d) * 2 + 1)
            greet(plane_at(d) * 2)
        greet(site - 1)

    lane = lax.broadcasted_iota(jnp.int32, (8, TILE), 1)
    first = jnp.full((8, TILE), TRIP, jnp.int32)
    second = first
    for k in reversed(range(TRIP)):
        hit = lane == owner_ref[outputs_ref[k]]
        second = jnp.where(hit, first, second)
        first = jnp.where(hit, k, first)
    upper = lax.broadcasted_iota(jnp.int32, (8, TILE), 0) == 0
    tables[site] = jnp.where(upper, first, second)

    own_bra.wait()
    for k in range(TRIP):
        turned = jnp.transpose(bra[k].astype(F32)) * weight_ref[terms_ref[k]]
        bt_out[:, k * ROWS:(k + 1) * ROWS, :] = turned.astype(BF16).reshape(NZ, ROWS, TILE)
    own_ket.wait()

    @pl.when(core == 0)
    def _():
        pl.semaphore_wait(barrier, N_COLUMN + 3 + jnp.where(z == 0, N_PLANE, 0))

        @pl.when(z == 0)
        def _():
            prod[TRIP] = jnp.zeros((ROWS, TILE), F32)
            fetch(0, 0).start()
            fetch(0, 0).wait()

            def chunk(c, carry):
                for h in range(WIDE):
                    products(bt_out[c * WIDE + h], env_ref[...], 0)
                    for i in range(SLOTS):
                        to = sector if i == N_PLANE else slot_at(PLANE[i])
                        first_out[c, i, h * ROWS:(h + 1) * ROWS] = summed(0, to)
                        if h == WIDE - 1:
                            send_first(c, i).start()
                return carry

            lax.fori_loop(0, NZ // WIDE, chunk, 0)
            out_ref[...] = env_ref[...]

        @pl.when(z > 0)
        def _():
            for d in COLUMN + [0]:
                send_table(d).start()

        def send_own(up, down):
            for q in range(PIECES):
                if up:
                    ket_piece(site, q, up_send, plane_at(1) * 2).start()
                if down:
                    held = kets.at[site, pl.ds(q * PIECE, PIECE)]
                    ket_piece(site, q, down_send, plane_at(NZ - 1) * 2).start()
                    remote(held, held, over_send, ket_recv.at[site, 0], z * 2 + 1).start()

        @pl.when(z == 1)
        def _():
            send_own(False, True)

        @pl.when(z > 0)
        def _():
            pl.semaphore_wait(gate, 1)

        @pl.when(z == 1)
        def _():
            send_own(True, False)

        @pl.when(z > 0)
        def _():
            for d in COLUMN + [0]:
                send_bt(d).start()

        def serve(f, carry):
            away = lax.rem(z - f // 2 + NZ, NZ)


            @pl.when(f != site)
            def _():
                for q in range(PIECES):
                    ket_piece(f, q, up_send, z * 2 + 1).wait_recv()
                    if 2 * q < PIECES:
                        up, down = away < NZ // 2, (away == 0) | (away > NZ // 2 + 1)
                    else:
                        up, down = away < NZ // 2 - 1, (away == 0) | (away > NZ // 2)
                    held = kets.at[f, pl.ds(q * PIECE, PIECE)]

                    @pl.when(up)
                    def _():
                        ket_piece(f, q, up_send, plane_at(1) * 2).start()

                    @pl.when(down)
                    def _():
                        ket_piece(f, q, down_send, plane_at(NZ - 1) * 2).start()

                    @pl.when(away > 0)
                    def _():
                        remote(held, held, over_send, ket_recv.at[f, 0], z * 2 + 1).start()

            @pl.when((f == jnp.minimum(site - 1, LEAD)) & (z > 1))
            def _():
                send_own(True, True)

            return carry

        lax.fori_loop(2, STEPS, serve, 0)

        @pl.when(z > 0)
        def _():
            to_core_0().wait_recv()
            out_ref[...] = land[...]

        def settle(f, carry):
            away = lax.rem(z - f // 2 + NZ, NZ)

            @pl.when(away < NZ // 2 - 1)
            def _():
                whole_ket(f, up_send).wait_send()

            @pl.when(away == NZ // 2 - 1)
            def _():
                whole_ket(f, up_send, TRIP // 2).wait_send()

            @pl.when((away == 0) | (away > NZ // 2 + 1))
            def _():
                whole_ket(f, down_send).wait_send()

            @pl.when(away == NZ // 2 + 1)
            def _():
                whole_ket(f, down_send, TRIP // 2).wait_send()

            @pl.when((away > 0) | (f == site))
            def _():
                whole_ket(f, over_send).wait_send()

            return carry

        lax.fori_loop(2, STEPS, settle, 0)
        @pl.when(z == 0)
        def _():
            remote(first_out, first_in, first_send, first_recv.at[0], 1).wait_send()

        @pl.when(z > 0)
        def _():
            for d in COLUMN + [0]:
                send_table(d).wait_send()
                send_bt(d).wait_send()

    @pl.when(core == 1)
    def _():
        prod[TRIP] = jnp.zeros((ROWS, TILE), F32)
        bt[site] = bt_out[z]
        pl.semaphore_wait(barrier, N_PLANE + N_COLUMN + jnp.where(z == 0, 0, 1))
        @pl.when(site < STEPS)
        def _():
            for d in COLUMN:
                send_table(d).start()

        @pl.when((site > 1) & (site < STEPS))
        def _():
            for q in range(PIECES):
                ket_piece(site, q, over_send, z * 2).start()

        def start_bt():
            for d in COLUMN:
                send_bt(d).start()

        half = PIECES // 2

        def first_kets(pieces, up, down, source=False):
            for q in pieces:
                for way, sem, d in ((up, up_send, 1), (down, down_send, NZ - 1)):
                    @pl.when(way)
                    def _():
                        if not source:
                            ket_piece(1, q, sem, site).wait_recv()
                        ket_piece(1, q, sem, plane_at(d) * 2 + 1).start()

        def take_kets(pieces):
            for q in pieces:
                ket_piece(1, q, up_send, site).wait_recv()

        first_kets(range(PIECES), z == 0, z == 0, source=True)

        @pl.when(site == 1)
        def _():
            start_bt()

        next_up, next_down = (z == 1) | (z == 2), (z == NZ - 1) | (z == NZ - 2)
        first_kets(range(half), next_up | (z == 3), next_down)
        first_kets(range(half, PIECES), next_up, next_down | (z == NZ - 3))

        @pl.when(z > 0)
        def _():
            pl.semaphore_signal(gate, inc=1, device_id=(z * 2, sector), device_id_type=MESH)

        @pl.when((z == 4) | (z == 5))
        def _():
            take_kets(range(half))

        @pl.when((z == 3) | (z == 4))
        def _():
            take_kets(range(half, PIECES))

        def send_part(p, i):
            return remote(
                part.at[p, i], got.at[p, i], part_send.at[p], part_recv.at[p, int(i >= N_FAR)],
                site, slot_at(PLANE[i]),
            )

        def some_parts(p, start, count, group=0):
            span = pl.ds(start, count)
            return remote(
                part.at[p, span], got.at[p, span], part_send.at[p], part_recv.at[p, group],
                site, slot_at(PLANE[0]),
            )

        def send_rows(q, d):
            held = env.at[q, rows]
            return remote(held, held, env_send.at[q], env_recv.at[q], plane_at(d) * 2 + 1)

        def all_rows(q):
            held = env.at[q, pl.ds(0, N_COLUMN * ROWS)]
            return remote(held, held, env_send.at[q], env_recv.at[q], plane_at(COLUMN[0]) * 2 + 1)

        def scatter(p):
            for i in range(N_PLANE):
                part[p, i] = summed(p, slot_at(PLANE[i]))
                send_part(p, i).start()
            got[p, N_PLANE] = summed(p, sector)

        def gather(p):
            some_parts(p, N_FAR, N_PLANE - N_FAR, 1).wait_recv()
            total = got[p, N_FAR].astype(F32)
            for i in range(N_FAR + 1, SLOTS):
                total += got[p, i].astype(F32)
            some_parts(p, 0, N_FAR).wait_recv()
            for i in range(N_FAR):
                total += got[p, i].astype(F32)
            env[1 - p, rows] = total.astype(BF16)
            for d in COLUMN:
                send_rows(1 - p, d).start()

        def fetch_table(j, p):
            @pl.when(j != site)
            def _():
                remote(tables.at[j], tables.at[j], table_send, table_recv.at[j], z * 2).wait_recv()

            fetch(j, p).start()

        fetch_table(1, 1)

        @pl.when(z == 0)
        def _():
            def chunk(c, carry):
                remote(first_in.at[c], first_in.at[c], first_send, first_recv.at[c], 0).wait_recv()
                total = first_in[c, 0].astype(F32)
                for i in range(1, SLOTS):
                    total += first_in[c, i].astype(F32)
                part_rows = pl.ds(pl.multiple_of(c * (WIDE * ROWS), WIDE * ROWS), WIDE * ROWS)
                env[1, part_rows] = total.astype(BF16)
                for d in COLUMN:
                    held = env.at[1, part_rows]
                    remote(held, held, env_send.at[1], env_recv.at[1], plane_at(d) * 2 + 1).start()
                return carry

            lax.fori_loop(0, NZ // WIDE, chunk, 0)

        def whole_env(q):
            return remote(env.at[q], env.at[q], env_send.at[q], env_recv.at[q], plane_at(1) * 2 + 1)

        @pl.when(z > 0)
        def _():
            whole_env(1).wait_recv()

        def step(j, carry):
            p = lax.rem(j, 2)

            @pl.when(j != site)
            def _():
                remote(bt.at[j], bt.at[j], bt_send, bt_recv.at[j], z * 2).wait_recv()

                @pl.when(j > 1)
                def _():
                    whole_ket(j, over_send).wait_recv()

            @pl.when(j > 1)
            def _():
                all_rows(p).wait_recv()

            products(bt[j], env[p], j)
            fetch(j, p).wait()
            scatter(p)

            @pl.when(j < STEPS - 1)
            def _():
                fetch_table(j + 1, 1 - p)

            @pl.when(j > 1)
            def _():
                some_parts(1 - p, 0, N_PLANE).wait_send()
                all_rows(p).wait_send()

            @pl.when((j == 1) & (z == 0))
            def _():
                for d in COLUMN:
                    whole_env(1).wait_send()

            @pl.when(j == z * 2)
            def _():
                leave[...] = env[p]
                to_core_0().start()

            @pl.when(j == site)
            def _():
                out_ref[...] = env[p]

            @pl.when((j == jnp.maximum(site - 2, 1)) & (site > 1) & (site < STEPS))
            def _():
                start_bt()

            gather(p)
            return carry

        lax.fori_loop(1, STEPS, step, 0)
        last = STEPS % 2
        all_rows(last).wait_recv()

        @pl.when(site == STEPS)
        def _():
            out_ref[...] = env[last]

        all_rows(last).wait_send()
        some_parts(1 - last, 0, N_PLANE).wait_send()

        @pl.when(z > 0)
        def _():
            to_core_0().wait_send()

        @pl.when(site < STEPS)
        def _():
            for d in COLUMN:
                send_table(d).wait_send()
                send_bt(d).wait_send()

        @pl.when((site > 1) & (site < STEPS))
        def _():
            whole_ket(site, over_send).wait_send()

        @pl.when(z < 3)
        def _():
            whole_ket(1, up_send).wait_send()

        @pl.when(z == 3)
        def _():
            whole_ket(1, up_send, TRIP // 2).wait_send()

        @pl.when((z == 0) | (z > 5))
        def _():
            whole_ket(1, down_send).wait_send()

        @pl.when(z == 5)
        def _():
            whole_ket(1, down_send, TRIP // 2).wait_send()


def run_chain(env, bra, ket, outputs, terms, owner, weight):
    vmem = pl.BlockSpec(memory_space=pltpu.VMEM)
    smem = pl.BlockSpec(memory_space=pltpu.SMEM)
    anywhere = pl.BlockSpec(memory_space=pl.ANY)
    dma = pltpu.SemaphoreType.DMA
    return pl.pallas_call(
        chain,
        out_shape=jax.ShapeDtypeStruct((TILE, TILE), BF16),
        in_specs=[vmem, anywhere, anywhere, smem, smem, smem, smem],
        out_specs=vmem,
        scratch_shapes=[
            pltpu.VMEM((TRIP, TILE, TILE), BF16),
            pltpu.VMEM((2, TILE, TILE), BF16),
            pltpu.VMEM((TRIP + 1, ROWS, TILE), F32),
            pltpu.VMEM((2, N_PLANE, ROWS, TILE), BF16),
            pltpu.VMEM((2, SLOTS, ROWS, TILE), BF16),
            pltpu.VMEM((TILE, TILE), BF16),
            pltpu.VMEM((TILE, TILE), BF16),
            pltpu.VMEM((NZ, TRIP * ROWS, TILE), BF16),
            pltpu.VMEM((2 * NZ, TRIP * ROWS, TILE), BF16),
            pltpu.VMEM((NZ // WIDE, SLOTS, WIDE * ROWS, TILE), BF16),
            pltpu.VMEM((NZ // WIDE, SLOTS, WIDE * ROWS, TILE), BF16),
            pltpu.VMEM((2 * NZ, TRIP, TILE, TILE), BF16),
            pltpu.VMEM((2 * NZ, 8, TILE), jnp.int32),
            pltpu.SMEM((2, 8, TILE), jnp.int32),
            dma((2,)), dma((2, 2)), dma((2,)), dma((2,)), dma, dma, dma, dma((2 * NZ,)),
            dma, dma((NZ,)), dma, dma((2 * NZ,)), dma((2,)), dma((2,)),
            dma, dma, dma, dma((2 * NZ, PIECES)),
            pltpu.SemaphoreType.REGULAR,
        ],
        compiler_params=pltpu.CompilerParams(
            collective_id=0, has_side_effects=True, vmem_limit_bytes=56 << 20
        ),
        name="chain",
    )(env, bra, ket, outputs, terms, owner, weight)


def local(left_env, mps_bra, mps_ket, joining_out, joining_mpo, owner, mpo_weight):
    envs = run_chain(
        left_env[0], mps_bra[0], mps_ket[0], joining_out[0, :, 0], joining_mpo[0], owner, mpo_weight[0]
    )
    return envs[None, None]


def solution(mesh):
    return jax.shard_map(
        local,
        mesh=mesh,
        in_specs=(
            P("sector", None, None),
            P("site", "sector", None, None),
            P("site", "sector", None, None),
            P("site", "sector", None),
            P("site", "sector"),
            P(),
            P("site", None),
        ),
        out_specs=P("site", "sector", None, None),
        check_vma=False,
    )
```

```python
import functools

import jax
import jax.numpy as jnp
from jax import lax
from jax.experimental import pallas as pl
from jax.experimental.pallas import tpu as pltpu
from jax.sharding import PartitionSpec as P

MESH = pl.DeviceIdType.MESH
BF16 = jnp.bfloat16
F32 = jnp.float32

NX, NY, NZ = 4, 8, 8
SLOTS = NX * NY
STEPS = 15
TRIP = 16
ROWS = 16
TILE = 128
PIECES = 16
PIECE = TRIP // PIECES
LEAD = 8
WIDE = 2


def hops(offset):
    dy, dx = offset
    return min(dy, NY - dy) + min(dx, NX - dx)


PLANE = sorted(
    [(dy, dx) for dy in range(NY) for dx in range(NX) if (dy, dx) != (0, 0)], key=hops, reverse=True
)
COLUMN = sorted(range(1, NZ), key=lambda d: min(d, NZ - d), reverse=True)
N_PLANE = len(PLANE)
N_COLUMN = len(COLUMN)
N_FAR = sum(hops(offset) > 4 for offset in PLANE)


def chain(
    env_ref, bra_ref, ket_ref, outputs_ref, terms_ref, owner_ref, weight_ref, out_ref,
    bra, env, prod, part, got, leave, land, bt_out, bt, first_out, first_in, kets, tables, lookup,
    part_send, part_recv, env_send, env_recv, out_send, out_recv, bt_send, bt_recv,
    first_send, first_recv, table_send, table_recv, table_sem, local_sem,
    up_send, down_send, over_send, ket_recv, gate,
):
    site = lax.axis_index("site")
    sector = lax.axis_index("sector")
    z, core = site // 2, lax.rem(site, 2)
    y, x = sector // NX, lax.rem(sector, NX)
    rows = pl.ds(pl.multiple_of(z * ROWS, ROWS), ROWS)

    def slot_at(offset):
        return lax.rem(y + offset[0], NY) * NX + lax.rem(x + offset[1], NX)

    def plane_at(d):
        return lax.rem(z + d, NZ)

    def remote(src, dst, send_sem, recv_sem, to_site, to_sector=sector):
        return pltpu.make_async_remote_copy(
            src_ref=src, dst_ref=dst, send_sem=send_sem, recv_sem=recv_sem,
            device_id=(to_site, to_sector), device_id_type=MESH,
        )

    barrier = pltpu.get_barrier_semaphore()

    def greet(to_site, to_sector=sector):
        pl.semaphore_signal(barrier, inc=1, device_id=(to_site, to_sector), device_id_type=MESH)

    def send_table(d):
        return remote(tables.at[site], tables.at[site], table_send, table_recv.at[site], plane_at(d) * 2 + 1)

    def send_bt(d):
        return remote(
            bt_out.at[plane_at(d)], bt.at[site], bt_send, bt_recv.at[site], plane_at(d) * 2 + 1
        )

    def send_first(c, i):
        to_sector = sector if i == N_PLANE else slot_at(PLANE[i])
        return remote(first_out.at[c, i], first_in.at[c, i], first_send, first_recv.at[c], 1, to_sector)

    def to_core_0():
        return remote(leave, land, out_send, out_recv, z * 2)

    def ket_piece(f, q, send_sem, to_site):
        held = kets.at[f, pl.ds(q * PIECE, PIECE)]
        return remote(held, held, send_sem, ket_recv.at[f, q], to_site)

    def whole_ket(f, send_sem, tiles=TRIP):
        held = kets.at[f, pl.ds(0, tiles)]
        return remote(held, held, send_sem, ket_recv.at[f, 0], site + 1 - 2 * core)

    own_ket = pltpu.make_async_copy(ket_ref, kets.at[site], local_sem.at[0])
    own_bra = pltpu.make_async_copy(bra_ref, bra, local_sem.at[1])
    own_ket.start()
    own_bra.start()
    def fetch(j, p):
        return pltpu.make_async_copy(tables.at[j], lookup.at[p], table_sem.at[p])

    def products(bt_chunk, block, j):
        left = jnp.dot(bt_chunk, block, preferred_element_type=F32).astype(BF16)
        for k in range(0, TRIP, 2):
            pair = jnp.concatenate([kets[j, k], kets[j, k + 1]], axis=1)
            both = jnp.dot(left[k * ROWS:(k + 2) * ROWS], pair, preferred_element_type=F32)
            prod[k] = both[:ROWS, :TILE]
            prod[k + 1] = both[ROWS:, TILE:]

    def summed(p, slot):
        return (prod[lookup[p, 0, slot]] + prod[lookup[p, 1, slot]]).astype(BF16)

    @pl.when(core == 0)
    def _():
        greet(plane_at(1) * 2)
        greet(plane_at(NZ - 1) * 2)

        @pl.when(z > 0)
        def _():
            greet(site + 1)

    @pl.when(core == 1)
    def _():
        for offset in PLANE:
            greet(site, slot_at(offset))

            @pl.when(z == 0)
            def _():
                greet(0, slot_at(offset))
        for d in COLUMN:
            greet(plane_at(d) * 2 + 1)
            greet(plane_at(d) * 2)
        greet(site - 1)

    lane = lax.broadcasted_iota(jnp.int32, (8, TILE), 1)
    first = jnp.full((8, TILE), TRIP, jnp.int32)
    second = first
    for k in reversed(range(TRIP)):
        hit = lane == owner_ref[outputs_ref[k]]
        second = jnp.where(hit, first, second)
        first = jnp.where(hit, k, first)
    upper = lax.broadcasted_iota(jnp.int32, (8, TILE), 0) == 0
    tables[site] = jnp.where(upper, first, second)

    def turn_bras():
        own_bra.wait()
        for k in range(TRIP):
            turned = jnp.transpose(bra[k].astype(F32)) * weight_ref[terms_ref[k]]
            bt_out[:, k * ROWS:(k + 1) * ROWS, :] = turned.astype(BF16).reshape(NZ, ROWS, TILE)

    own_ket.wait()

    @pl.when(core == 0)
    def _():
        turn_bras()
        pl.semaphore_wait(barrier, N_COLUMN + 3 + jnp.where(z == 0, N_PLANE, 0))

        @pl.when(z == 0)
        def _():
            prod[TRIP] = jnp.zeros((ROWS, TILE), F32)
            fetch(0, 0).start()
            fetch(0, 0).wait()

            def chunk(c, carry):
                for h in range(WIDE):
                    products(bt_out[c * WIDE + h], env_ref[...], 0)
                    for i in range(SLOTS):
                        to = sector if i == N_PLANE else slot_at(PLANE[i])
                        first_out[c, i, h * ROWS:(h + 1) * ROWS] = summed(0, to)
                        if h == WIDE - 1:
                            send_first(c, i).start()
                return carry

            lax.fori_loop(0, NZ // WIDE, chunk, 0)
            out_ref[...] = env_ref[...]

        @pl.when(z > 0)
        def _():
            for d in COLUMN + [0]:
                send_table(d).start()

        def send_own(up, down):
            for q in range(PIECES):
                if up:
                    ket_piece(site, q, up_send, plane_at(1) * 2).start()
                if down:
                    held = kets.at[site, pl.ds(q * PIECE, PIECE)]
                    ket_piece(site, q, down_send, plane_at(NZ - 1) * 2).start()
                    remote(held, held, over_send, ket_recv.at[site, 0], z * 2 + 1).start()

        @pl.when(z == 1)
        def _():
            send_own(False, True)

        @pl.when(z > 0)
        def _():
            pl.semaphore_wait(gate, 1)

        @pl.when(z == 1)
        def _():
            send_own(True, False)

        @pl.when(z > 0)
        def _():
            for d in COLUMN + [0]:
                send_bt(d).start()

        def serve(f, carry):
            away = lax.rem(z - f // 2 + NZ, NZ)


            @pl.when(f != site)
            def _():
                for q in range(PIECES):
                    ket_piece(f, q, up_send, z * 2 + 1).wait_recv()
                    if 2 * q < PIECES:
                        up, down = away < NZ // 2, (away == 0) | (away > NZ // 2 + 1)
                    else:
                        up, down = away < NZ // 2 - 1, (away == 0) | (away > NZ // 2)
                    held = kets.at[f, pl.ds(q * PIECE, PIECE)]

                    @pl.when(up)
                    def _():
                        ket_piece(f, q, up_send, plane_at(1) * 2).start()

                    @pl.when(down)
                    def _():
                        ket_piece(f, q, down_send, plane_at(NZ - 1) * 2).start()

                    @pl.when(away > 0)
                    def _():
                        remote(held, held, over_send, ket_recv.at[f, 0], z * 2 + 1).start()

            @pl.when((f == jnp.minimum(site - 1, LEAD)) & (z > 1))
            def _():
                send_own(True, True)

            return carry

        lax.fori_loop(2, STEPS, serve, 0)

        @pl.when(z > 0)
        def _():
            to_core_0().wait_recv()
            out_ref[...] = land[...]

        def settle(f, carry):
            away = lax.rem(z - f // 2 + NZ, NZ)

            @pl.when(away < NZ // 2 - 1)
            def _():
                whole_ket(f, up_send).wait_send()

            @pl.when(away == NZ // 2 - 1)
            def _():
                whole_ket(f, up_send, TRIP // 2).wait_send()

            @pl.when((away == 0) | (away > NZ // 2 + 1))
            def _():
                whole_ket(f, down_send).wait_send()

            @pl.when(away == NZ // 2 + 1)
            def _():
                whole_ket(f, down_send, TRIP // 2).wait_send()

            @pl.when((away > 0) | (f == site))
            def _():
                whole_ket(f, over_send).wait_send()

            return carry

        lax.fori_loop(2, STEPS, settle, 0)
        @pl.when(z == 0)
        def _():
            remote(first_out, first_in, first_send, first_recv.at[0], 1).wait_send()

        @pl.when(z > 0)
        def _():
            for d in COLUMN + [0]:
                send_table(d).wait_send()
                send_bt(d).wait_send()

    @pl.when(core == 1)
    def _():
        prod[TRIP] = jnp.zeros((ROWS, TILE), F32)
        pl.semaphore_wait(barrier, N_PLANE + N_COLUMN + jnp.where(z == 0, 0, 1))
        @pl.when(site < STEPS)
        def _():
            for d in COLUMN:
                send_table(d).start()

        @pl.when((site > 1) & (site < STEPS))
        def _():
            for q in range(PIECES):
                ket_piece(site, q, over_send, z * 2).start()

        def start_bt():
            for d in COLUMN:
                send_bt(d).start()

        half = PIECES // 2

        def first_kets(pieces, up, down, source=False):
            for q in pieces:
                for way, sem, d in ((up, up_send, 1), (down, down_send, NZ - 1)):
                    @pl.when(way)
                    def _():
                        if not source:
                            ket_piece(1, q, sem, site).wait_recv()
                        ket_piece(1, q, sem, plane_at(d) * 2 + 1).start()

        def take_kets(pieces):
            for q in pieces:
                ket_piece(1, q, up_send, site).wait_recv()

        first_kets(range(PIECES), z == 0, z == 0, source=True)
        turn_bras()
        bt[site] = bt_out[z]

        @pl.when(site == 1)
        def _():
            start_bt()

        next_up, next_down = (z == 1) | (z == 2), (z == NZ - 1) | (z == NZ - 2)
        first_kets(range(half), next_up | (z == 3), next_down)
        first_kets(range(half, PIECES), next_up, next_down | (z == NZ - 3))

        @pl.when(z > 0)
        def _():
            pl.semaphore_signal(gate, inc=1, device_id=(z * 2, sector), device_id_type=MESH)

        @pl.when((z == 4) | (z == 5))
        def _():
            take_kets(range(half))

        @pl.when((z == 3) | (z == 4))
        def _():
            take_kets(range(half, PIECES))

        def send_part(p, i):
            return remote(
                part.at[p, i], got.at[p, i], part_send.at[p], part_recv.at[p, int(i >= N_FAR)],
                site, slot_at(PLANE[i]),
            )

        def some_parts(p, start, count, group=0):
            span = pl.ds(start, count)
            return remote(
                part.at[p, span], got.at[p, span], part_send.at[p], part_recv.at[p, group],
                site, slot_at(PLANE[0]),
            )

        def send_rows(q, d):
            held = env.at[q, rows]
            return remote(held, held, env_send.at[q], env_recv.at[q], plane_at(d) * 2 + 1)

        def all_rows(q):
            held = env.at[q, pl.ds(0, N_COLUMN * ROWS)]
            return remote(held, held, env_send.at[q], env_recv.at[q], plane_at(COLUMN[0]) * 2 + 1)

        def scatter(p):
            for i in range(N_PLANE):
                part[p, i] = summed(p, slot_at(PLANE[i]))
                send_part(p, i).start()
            got[p, N_PLANE] = summed(p, sector)

        def gather(p):
            some_parts(p, N_FAR, N_PLANE - N_FAR, 1).wait_recv()
            total = got[p, N_FAR].astype(F32)
            for i in range(N_FAR + 1, SLOTS):
                total += got[p, i].astype(F32)
            some_parts(p, 0, N_FAR).wait_recv()
            for i in range(N_FAR):
                total += got[p, i].astype(F32)
            env[1 - p, rows] = total.astype(BF16)
            for d in COLUMN:
                send_rows(1 - p, d).start()

        def fetch_table(j, p):
            @pl.when(j != site)
            def _():
                remote(tables.at[j], tables.at[j], table_send, table_recv.at[j], z * 2).wait_recv()

            fetch(j, p).start()

        fetch_table(1, 1)

        @pl.when(z == 0)
        def _():
            def chunk(c, carry):
                remote(first_in.at[c], first_in.at[c], first_send, first_recv.at[c], 0).wait_recv()
                total = first_in[c, 0].astype(F32)
                for i in range(1, SLOTS):
                    total += first_in[c, i].astype(F32)
                part_rows = pl.ds(pl.multiple_of(c * (WIDE * ROWS), WIDE * ROWS), WIDE * ROWS)
                env[1, part_rows] = total.astype(BF16)
                for d in COLUMN:
                    held = env.at[1, part_rows]
                    remote(held, held, env_send.at[1], env_recv.at[1], plane_at(d) * 2 + 1).start()
                return carry

            lax.fori_loop(0, NZ // WIDE, chunk, 0)

        def whole_env(q):
            return remote(env.at[q], env.at[q], env_send.at[q], env_recv.at[q], plane_at(1) * 2 + 1)

        @pl.when(z > 0)
        def _():
            whole_env(1).wait_recv()

        def step(j, carry):
            p = lax.rem(j, 2)

            @pl.when(j != site)
            def _():
                remote(bt.at[j], bt.at[j], bt_send, bt_recv.at[j], z * 2).wait_recv()

                @pl.when(j > 1)
                def _():
                    whole_ket(j, over_send).wait_recv()

            @pl.when(j > 1)
            def _():
                all_rows(p).wait_recv()

            products(bt[j], env[p], j)
            fetch(j, p).wait()
            scatter(p)

            @pl.when(j < STEPS - 1)
            def _():
                fetch_table(j + 1, 1 - p)

            @pl.when(j > 1)
            def _():
                some_parts(1 - p, 0, N_PLANE).wait_send()
                all_rows(p).wait_send()

            @pl.when((j == 1) & (z == 0))
            def _():
                for d in COLUMN:
                    whole_env(1).wait_send()

            @pl.when(j == z * 2)
            def _():
                leave[...] = env[p]
                to_core_0().start()

            @pl.when(j == site)
            def _():
                out_ref[...] = env[p]

            @pl.when((j == jnp.maximum(site - 2, 1)) & (site > 1) & (site < STEPS))
            def _():
                start_bt()

            gather(p)
            return carry

        lax.fori_loop(1, STEPS, step, 0)
        last = STEPS % 2
        all_rows(last).wait_recv()

        @pl.when(site == STEPS)
        def _():
            out_ref[...] = env[last]

        all_rows(last).wait_send()
        some_parts(1 - last, 0, N_PLANE).wait_send()

        @pl.when(z > 0)
        def _():
            to_core_0().wait_send()

        @pl.when(site < STEPS)
        def _():
            for d in COLUMN:
                send_table(d).wait_send()
                send_bt(d).wait_send()

        @pl.when((site > 1) & (site < STEPS))
        def _():
            whole_ket(site, over_send).wait_send()

        @pl.when(z < 3)
        def _():
            whole_ket(1, up_send).wait_send()

        @pl.when(z == 3)
        def _():
            whole_ket(1, up_send, TRIP // 2).wait_send()

        @pl.when((z == 0) | (z > 5))
        def _():
            whole_ket(1, down_send).wait_send()

        @pl.when(z == 5)
        def _():
            whole_ket(1, down_send, TRIP // 2).wait_send()


def run_chain(env, bra, ket, outputs, terms, owner, weight):
    vmem = pl.BlockSpec(memory_space=pltpu.VMEM)
    smem = pl.BlockSpec(memory_space=pltpu.SMEM)
    anywhere = pl.BlockSpec(memory_space=pl.ANY)
    dma = pltpu.SemaphoreType.DMA
    return pl.pallas_call(
        chain,
        out_shape=jax.ShapeDtypeStruct((TILE, TILE), BF16),
        in_specs=[vmem, anywhere, anywhere, smem, smem, smem, smem],
        out_specs=vmem,
        scratch_shapes=[
            pltpu.VMEM((TRIP, TILE, TILE), BF16),
            pltpu.VMEM((2, TILE, TILE), BF16),
            pltpu.VMEM((TRIP + 1, ROWS, TILE), F32),
            pltpu.VMEM((2, N_PLANE, ROWS, TILE), BF16),
            pltpu.VMEM((2, SLOTS, ROWS, TILE), BF16),
            pltpu.VMEM((TILE, TILE), BF16),
            pltpu.VMEM((TILE, TILE), BF16),
            pltpu.VMEM((NZ, TRIP * ROWS, TILE), BF16),
            pltpu.VMEM((2 * NZ, TRIP * ROWS, TILE), BF16),
            pltpu.VMEM((NZ // WIDE, SLOTS, WIDE * ROWS, TILE), BF16),
            pltpu.VMEM((NZ // WIDE, SLOTS, WIDE * ROWS, TILE), BF16),
            pltpu.VMEM((2 * NZ, TRIP, TILE, TILE), BF16),
            pltpu.VMEM((2 * NZ, 8, TILE), jnp.int32),
            pltpu.SMEM((2, 8, TILE), jnp.int32),
            dma((2,)), dma((2, 2)), dma((2,)), dma((2,)), dma, dma, dma, dma((2 * NZ,)),
            dma, dma((NZ,)), dma, dma((2 * NZ,)), dma((2,)), dma((2,)),
            dma, dma, dma, dma((2 * NZ, PIECES)),
            pltpu.SemaphoreType.REGULAR,
        ],
        compiler_params=pltpu.CompilerParams(
            collective_id=0, has_side_effects=True, vmem_limit_bytes=56 << 20
        ),
        name="chain",
    )(env, bra, ket, outputs, terms, owner, weight)


def local(left_env, mps_bra, mps_ket, joining_out, joining_mpo, owner, mpo_weight):
    envs = run_chain(
        left_env[0], mps_bra[0], mps_ket[0], joining_out[0, :, 0], joining_mpo[0], owner, mpo_weight[0]
    )
    return envs[None, None]


def solution(mesh):
    return jax.shard_map(
        local,
        mesh=mesh,
        in_specs=(
            P("sector", None, None),
            P("site", "sector", None, None),
            P("site", "sector", None, None),
            P("site", "sector", None),
            P("site", "sector"),
            P(),
            P("site", None),
        ),
        out_specs=P("site", "sector", None, None),
        check_vma=False,
    )
```
